256 devices in a mesh: blk: 16 (over x_lo, z), red: 16 (over x_hi, y, core).
Axes of the slice: x: 4 (x_hi: 2, x_lo: 2; x = x_hi * 2 + x_lo), y: 4, z: 8, core: 2. Of those that a mesh axis runs over, the one named last changes fastest.
Arguments:
- resid: float32 [1024, 16384], P('blk', 'red'), may hold values from -64 to 64
- norm_gain: float32 [16384], P('red'), may hold values from 0.1 to 1.9
- w_query: bfloat16 [16384, 16384], P('red', 'blk'), may hold values from -0.046875 to 0.046875
- w_key: bfloat16 [16384, 1024], P('red'), may hold values from -0.046875 to 0.046875
- w_value: bfloat16 [16384, 1024], P('red'), may hold values from -0.046875 to 0.046875
- w_out: bfloat16 [16384, 16384], P('blk', 'red'), may hold values from -0.046875 to 0.046875
- cache_key: bfloat16 [8192, 1024], P('red'), may hold values from -512 to 512
- cache_value: bfloat16 [8192, 1024], P('red'), may hold values from -8 to 8
- prefix_len: int32 [1], replicated, may hold values from 4096 to 8192
Outputs:
- updated: float32 [1024, 16384], P('blk', 'red')
The draws below stay inside these ranges and needn't reach their ends.
Inputs may be any that keep to these rules, and one draw needn't show every extreme that they name: `prefix_len`: cache slots below it hold the sequence's earlier tokens; the others are unused.
All inputs are finite; a program needn't handle non-finite values.
Results may differ from the reference program's by a relative error of at most 0.003.
The reference program's roundings to bfloat16 on the way count: a program that leaves them out, or rounds other values in their place, can miss the bound.
Values may be sent and summed in bfloat16 or wider, within the bound.
A program may use at most 192 MiB of HBM per device.

```python
import math
import jax
import jax.numpy as jnp
from jax import lax

D = 16384
H = 128
KV = 8
HD = 128
SPAN = 1024
CACHE = 8192


def region_table(key, width):
    regions = jnp.arange(CACHE, dtype=jnp.int32) * 16 // CACHE
    table = jax.random.truncated_normal(key, -4.0, 4.0, (16, width), dtype=jnp.float32)
    return table[regions]


def draw_resid(key, part):
    key = jax.random.fold_in(key, 11)
    key_rows, key_cols, key_base = jax.random.split(key, 3)
    rows = jnp.exp(jax.random.uniform(key_rows, (SPAN, 1), jnp.float32, math.log(0.3), math.log(3.0)))
    cols = jnp.exp(jax.random.uniform(key_cols, (1, D), jnp.float32, math.log(0.5), math.log(2.0)))
    cols = cols * (1.0 + jnp.arange(D, dtype=jnp.float32)[None, :] / D)
    base = jax.random.truncated_normal(key_base, -4.0, 4.0, (SPAN, D), dtype=jnp.float32)
    return base * rows * cols


def draw_cache_key(key, part):
    key = jax.random.fold_in(key, 23)
    key_table, key_noise = jax.random.split(key, 2)
    width = KV * HD
    offsets = region_table(key_table, width)
    noise = jax.random.truncated_normal(key_noise, -4.0, 4.0, (CACHE, width), dtype=jnp.float32)
    keys = 0.7 * noise + 0.7 * offsets
    return keys.astype(jnp.bfloat16)


def draw_cache_value(key, part):
    key = jax.random.fold_in(key, 37)
    key_table, key_noise = jax.random.split(key, 2)
    width = KV * HD
    offsets = region_table(key_table, width)
    noise = jax.random.truncated_normal(key_noise, -4.0, 4.0, (CACHE, width), dtype=jnp.float32)
    return (0.6 * noise + offsets).astype(jnp.bfloat16)


def block_levels(rng, shape, cuts, low, top_value):
    level = 1.0
    for axis_at, parts in cuts:
        steps = jax.random.uniform(jax.random.fold_in(jax.random.fold_in(rng, 6), axis_at), (parts,), jnp.float32, low / len(cuts), top_value / len(cuts))
        level = level * jnp.repeat(jnp.exp(steps), shape[axis_at] // parts).reshape((-1,) + (1,) * (len(shape) - 1 - axis_at))
    return level


def centred(stream_key, dims, scale, limit, cuts=(), kind=jnp.bfloat16):
    drawn = jax.random.normal(stream_key, dims, jnp.float32) * scale
    if len(cuts) > 0:
        drawn = block_levels(stream_key, dims, cuts, -0.22, 0.18) * drawn
    return jnp.clip(drawn, min=-limit, max=limit).astype(kind)


def setup_inputs(seed: int = 0) -> dict:
    streams_of = jax.random.split(jax.random.key(seed), 10)
    resid = draw_resid(jax.random.fold_in(streams_of[9], 71), 0)
    norm_gain = jnp.clip(1.0 + 0.18 * jax.random.normal(streams_of[1], (D,), jnp.float32), 0.1, 1.9)
    w_query = centred(streams_of[2], (D, H * HD), D ** -0.5, 0.046875, ((0, 16), (1, 16)))
    w_key = centred(streams_of[3], (D, KV * HD), D ** -0.5, 0.046875, ((0, 16),))
    w_value = centred(streams_of[4], (D, KV * HD), D ** -0.5, 0.046875, ((0, 16),))
    w_out = centred(streams_of[5], (H * HD, D), (H * HD) ** -0.5, 0.046875, ((0, 16), (1, 16)))
    cache_key = draw_cache_key(jax.random.fold_in(streams_of[9], 71), 0)
    cache_value = draw_cache_value(jax.random.fold_in(streams_of[9], 71), 0)
    prefix_len = jax.random.randint(streams_of[8], (1,), CACHE // 2, CACHE + 1).astype(jnp.int32)
    return dict(resid=resid, norm_gain=norm_gain, w_query=w_query, w_key=w_key, w_value=w_value, w_out=w_out, cache_key=cache_key, cache_value=cache_value, prefix_len=prefix_len)


theta = 500000.0

def rotate(values, positions):
    half = values.shape[-1] // 2
    steps = jnp.arange(half, dtype=jnp.float32)
    freq = theta ** (-(steps * 2.0) / values.shape[-1])
    angle = positions.astype(jnp.float32)[:, None] * freq[None, :]
    cosine = jnp.cos(angle)[:, None, :]
    sine = jnp.sin(angle)[:, None, :]
    first = values[..., :half]
    second = values[..., half:]
    return jnp.concatenate([first * cosine - second * sine, second * cosine + first * sine], axis=-1)

def reference(resid, norm_gain, w_query, w_key, w_value, w_out, cache_key, cache_value, prefix_len):
    meansq = lax.optimization_barrier(jnp.mean(resid * resid, axis=1, keepdims=True))
    normed = (resid * lax.rsqrt(meansq + 1e-05) * norm_gain[None, :]).astype(jnp.bfloat16)
    query_raw = jnp.dot(normed, w_query, preferred_element_type=jnp.float32)
    key_raw = jnp.dot(normed, w_key, preferred_element_type=jnp.float32)
    value = jnp.dot(normed, w_value, preferred_element_type=jnp.float32).astype(jnp.bfloat16)
    start = prefix_len[0]
    positions = start + jnp.arange(SPAN, dtype=jnp.int32)
    query = rotate(query_raw.reshape(SPAN, H, HD), positions).astype(jnp.bfloat16)
    key = rotate(key_raw.reshape(SPAN, KV, HD), positions).astype(jnp.bfloat16)
    value = value.reshape(SPAN, KV, HD)
    old_keys = cache_key.reshape(CACHE, KV, HD)
    old_values = cache_value.reshape(CACHE, KV, HD)
    group = H // KV
    scale = HD ** (-0.5)
    cache_ok = (jnp.arange(CACHE, dtype=jnp.int32) < start)[None, None, :]
    every = jnp.arange(SPAN, dtype=jnp.int32)
    causal = (every[None, :] <= every[:, None])[:, None, :]

    def one_group(index):
        heads = lax.dynamic_slice_in_dim(query, index * group, group, 1).astype(jnp.float32)
        ok_keys = lax.dynamic_slice_in_dim(old_keys, index, 1, 1)[:, 0, :].astype(jnp.float32)
        ok_vals = lax.dynamic_slice_in_dim(old_values, index, 1, 1)[:, 0, :].astype(jnp.float32)
        new_keys = lax.dynamic_slice_in_dim(key, index, 1, 1)[:, 0, :].astype(jnp.float32)
        new_vals = lax.dynamic_slice_in_dim(value, index, 1, 1)[:, 0, :].astype(jnp.float32)
        old_scores = jnp.einsum('tgd,cd->tgc', heads, ok_keys) * scale
        new_scores = jnp.einsum('tgd,sd->tgs', heads, new_keys) * scale
        peak = jnp.maximum(lax.optimization_barrier(jnp.max(jnp.where(cache_ok, old_scores, -1e+30), axis=2)), lax.optimization_barrier(jnp.max(jnp.where(causal, new_scores, -1e+30), axis=2)))
        old_w = jnp.where(cache_ok, jnp.exp(old_scores - peak[:, :, None]), 0.0).astype(jnp.bfloat16).astype(jnp.float32)
        new_w = jnp.where(causal, jnp.exp(new_scores - peak[:, :, None]), 0.0).astype(jnp.bfloat16).astype(jnp.float32)
        total = lax.optimization_barrier(jnp.sum(old_w, axis=2)) + lax.optimization_barrier(jnp.sum(new_w, axis=2))
        mixed = jnp.einsum('tgc,cd->tgd', old_w, ok_vals) + jnp.einsum('tgs,sd->tgd', new_w, new_vals)
        return (mixed / total[:, :, None]).astype(jnp.bfloat16)
    blocks = lax.map(one_group, jnp.arange(KV, dtype=jnp.int32))
    attention = jnp.transpose(blocks, (1, 0, 2, 3)).reshape(SPAN, H * HD)
    return resid + jnp.dot(attention, w_out, preferred_element_type=jnp.float32)
```

```python
import functools
import math

import jax
import jax.numpy as jnp
from jax import lax
from jax.experimental import pallas as pl
from jax.experimental.pallas import tpu as pltpu
from jax.sharding import PartitionSpec as P

MESH = pl.DeviceIdType.MESH
F32, BF16, I16, I32 = jnp.float32, jnp.bfloat16, jnp.int16, jnp.int32

HD = 128
THETA = 500000.0
ROWS = 64
WIDE = 1024
PROJ = WIDE + 2 * HD
SLOTS = 512
CACHE = 8192
SPAN = 1024
KEYS = CACHE + SPAN
CHUNK = 1024
HALF = 256
STEP = 8.0
TOP = 32000.0
NEG = -1e30


def rem(a, n):
    return lax.rem(a, jnp.int32(n))


def quantize(dst, v):
    n = v.shape[1]
    fold = jnp.abs(v[:, :HD])
    for k in range(1, n // HD):
        fold = jnp.maximum(fold, jnp.abs(v[:, k * HD : (k + 1) * HD]))
    top = jnp.max(fold, axis=1, keepdims=True)
    e = jnp.ceil(jnp.log2(jnp.maximum(top, 1e-30)) * STEP)
    e = jnp.broadcast_to(e, (v.shape[0], HD))
    up = jnp.exp2(e * (-1.0 / STEP)) * TOP
    for k in range(n // HD):
        dst[:, k * HD : (k + 1) * HD] = jnp.round(v[:, k * HD : (k + 1) * HD] * up).astype(I32).astype(I16)
    dst[:, n : n + HD] = e.astype(I32).astype(I16)


def restore(src, n):
    e = src[:, n : n + HD].astype(I32).astype(F32)
    down = jnp.exp2(e * (1.0 / STEP)) * (1.0 / TOP)
    return jnp.concatenate(
        [src[:, k * HD : (k + 1) * HD].astype(I32).astype(F32) * down for k in range(n // HD)], axis=1
    )


def kernel(
    start_ref, resid_hbm, gain_ref, wq_hbm, wk_hbm, wv_hbm, wo_hbm, ck_hbm, cv_hbm, cos_ref, sin_ref,
    out_ref,
    res, w, wo, g, kv, pb, sq, pp, sib, qs, qr, acc, qh, s_ref, mix, att, op, xs, xr, zs, zr,
    load_sem, sq_send, sq_recv, ag_send, ag_recv, kv_send, kv_recv, sib_send, sib_recv, qs_send, qr_recv,
    nk_send, nk_recv, at_send, at_recv, xs_send, xr_recv, zs_send, zr_recv,
):
    b = lax.axis_index("blk")
    r = lax.axis_index("red")
    xl, z = lax.div(b, jnp.int32(8)), rem(b, 8)
    xh, y, c = lax.div(r, jnp.int32(8)), rem(lax.div(r, jnp.int32(2)), 4), rem(r, 2)
    chip = lax.div(r, jnp.int32(2))
    head = lax.div(b, jnp.int32(2))

    def blk_of(px, pz):
        return px * 8 + rem(pz + 16, 8)

    def red_of(px, py, pc):
        return (px * 4 + rem(py + 8, 4)) * 2 + pc

    z_up, z_down = (blk_of(xl, z + 1), r), (blk_of(xl, z - 1), r)
    x_pair = (blk_of(1 - xl, z), r)
    x_across = (blk_of(1 - xl, z), red_of(1 - xh, y, c))
    sibling = (b, red_of(xh, y, 1 - c))

    barrier = pltpu.get_barrier_semaphore()
    peers = [(b, rem(r + i, 16)) for i in range(1, 16)] + [z_up, z_down, x_pair, x_across]
    for p in peers:
        pl.semaphore_signal(barrier, inc=1, device_id=p, device_id_type=MESH)

    mine = pl.ds(pl.multiple_of(r * SLOTS, SLOTS), SLOTS)
    my_cols = pl.ds(pl.multiple_of(head * HD, HD), HD)
    pair_head = lax.div(blk_of(1 - xl, z), jnp.int32(2))
    pair_cols = pl.ds(pl.multiple_of(pair_head * HD, HD), HD)
    loads = [
        pltpu.make_async_copy(resid_hbm, res, load_sem.at[0]),
        pltpu.make_async_copy(ck_hbm.at[:, my_cols], kv.at[mine, 0:HD], load_sem.at[1]),
        pltpu.make_async_copy(cv_hbm.at[:, my_cols], kv.at[mine, HD : 2 * HD], load_sem.at[2]),
        pltpu.make_async_copy(ck_hbm.at[:, pair_cols], pb.at[:, 0:HD], load_sem.at[3]),
        pltpu.make_async_copy(cv_hbm.at[:, pair_cols], pb.at[:, HD : 2 * HD], load_sem.at[4]),
        pltpu.make_async_copy(wq_hbm, w.at[:, 0:WIDE], load_sem.at[5]),
        pltpu.make_async_copy(wk_hbm.at[:, my_cols], w.at[:, WIDE : WIDE + HD], load_sem.at[6]),
        pltpu.make_async_copy(wv_hbm.at[:, my_cols], w.at[:, WIDE + HD : PROJ], load_sem.at[7]),
        pltpu.make_async_copy(wo_hbm, wo, load_sem.at[8]),
    ]
    for cp in loads:
        cp.start()

    sends = []

    def send(src, dst, ssem, rsem, to):
        cp = pltpu.make_async_remote_copy(
            src_ref=src, dst_ref=dst, send_sem=ssem, recv_sem=rsem, device_id=to, device_id_type=MESH
        )
        cp.start()
        sends.append(cp)

    def arrived(dst, rsem):
        pltpu.make_async_remote_copy(
            src_ref=dst, dst_ref=dst, send_sem=load_sem.at[0], recv_sem=rsem, device_id=sibling, device_id_type=MESH
        ).wait_recv()

    loads[0].wait()
    fold = jnp.zeros((ROWS, HD), F32)
    for k in range(WIDE // HD):
        v = res[:, k * HD : (k + 1) * HD]
        fold = fold + v * v
    square = jnp.concatenate([fold, jnp.zeros((HD - ROWS, HD), F32)], axis=0).T
    sq[r] = jnp.broadcast_to(jnp.sum(square, axis=0, keepdims=True), (8, HD))
    pl.semaphore_wait(barrier, len(peers))
    for i in range(1, 16):
        send(sq.at[r], sq.at[r], sq_send.at[i], sq_recv.at[r], (b, rem(r + i, 16)))

    for cp in loads[1:5]:
        cp.wait()

    def kv_rows(red):
        return kv.at[pl.ds(pl.multiple_of(red * SLOTS, SLOTS), SLOTS), 0 : 2 * HD]

    kv_count = [0]

    def kv_send_to(red, to, src=None):
        send(kv_rows(red) if src is None else src, kv_rows(red), kv_send.at[kv_count[0]], kv_recv.at[red], to)
        kv_count[0] += 1

    kv_send_to(r, x_across, src=pb)
    for d in (1, 3, 2):
        kv_send_to(r, (b, red_of(xh, y + d, c)))
    kv_send_to(r, sibling)

    kv[:, 2 * HD : 3 * HD] = jnp.ones((KEYS, HD), BF16)

    for i in range(1, 16):
        p = rem(r + i, 16)
        arrived(sq.at[p], sq_recv.at[p])
    total = jnp.sum(sq[...], axis=0)[0:1]
    column = jnp.broadcast_to(total, (HD, HD)).T[:ROWS]
    factor = lax.rsqrt(column / (WIDE * 16.0) + 1e-05)
    for k in range(WIDE // HD):
        lanes = slice(k * HD, (k + 1) * HD)
        g[b, :, lanes] = (res[:, lanes] * factor * gain_ref[:, lanes]).astype(BF16)

    ag_count = [0]

    def g_send(px, pz, to):
        slot = blk_of(px, pz)
        send(g.at[slot], g.at[slot], ag_send.at[ag_count[0]], ag_recv.at[slot], to)
        ag_count[0] += 1

    def g_wait(px, pz):
        slot = blk_of(px, pz)
        arrived(g.at[slot], ag_recv.at[slot])

    ox = 1 - xl
    g_send(xl, z, z_up)
    g_send(xl, z, z_down)
    g_send(xl, z, x_pair)
    g_wait(ox, z)
    g_send(ox, z, z_up)
    g_send(ox, z, z_down)
    g_wait(xl, z - 1)
    g_send(xl, z - 1, z_up)
    g_wait(xl, z + 1)
    g_send(xl, z + 1, z_down)
    r_across = red_of(1 - xh, y, c)
    arrived(kv_rows(r_across), kv_recv.at[r_across])
    for d in (1, 3, 2):
        kv_send_to(r_across, (b, red_of(xh, y + d, c)))
    kv_send_to(r_across, sibling)
    g_wait(ox, z - 1)
    g_send(ox, z - 1, z_up)
    g_wait(ox, z + 1)
    g_send(ox, z + 1, z_down)
    g_wait(xl, z - 2)
    g_send(xl, z - 2, z_up)
    g_wait(xl, z + 2)
    g_send(xl, z + 2, z_down)
    for d in (1, 3):
        red = red_of(xh, y + d, c)
        arrived(kv_rows(red), kv_recv.at[red])
        kv_send_to(red, sibling)
    g_wait(xl, z - 3)
    g_send(xl, z - 3, z_up)
    g_send(xl, z - 3, x_pair)
    g_wait(xl, z + 3)
    g_send(xl, z + 3, x_pair)
    g_wait(ox, z - 2)
    g_wait(ox, z + 2)
    g_wait(xl, z - 4)
    g_send(xl, z - 4, x_pair)
    g_wait(ox, z - 3)
    g_wait(ox, z + 3)
    g_wait(ox, z - 4)

    for cp in loads[5:8]:
        cp.wait()

    def to_sibling(i):
        return pltpu.make_async_remote_copy(
            src_ref=pp.at[i, 1 - c], dst_ref=sib.at[i], send_sem=sib_send.at[i], recv_sem=sib_recv.at[i],
            device_id=sibling, device_id_type=MESH,
        )

    def to_chip(i):
        j = rem(chip + 1 + i, 8)
        return pltpu.make_async_remote_copy(
            src_ref=qs.at[i], dst_ref=qr.at[chip], send_sem=qs_send.at[i], recv_sem=qr_recv.at[chip],
            device_id=(b, j * 2 + c), device_id_type=MESH,
        )

    def pass_on(i):
        to_sibling(i).wait_recv()
        quantize(qs.at[i], pp[i, c] + sib[i])
        to_chip(i).start()

    def project(i, _):
        j = rem(chip + 1 + i, 8)
        x = g[pl.ds(j * 2, 2)].reshape(2 * ROWS, WIDE)
        for n in range(PROJ // 256):
            t = jnp.dot(x, w[:, n * 256 : (n + 1) * 256], preferred_element_type=F32)
            pp[i, :, :, n * 256 : (n + 1) * 256] = t.reshape(2, ROWS, 256)
        to_sibling(i).start()

        @pl.when(i > 0)
        def _():
            pass_on(i - 1)

        return 0

    lax.fori_loop(0, 8, project, 0)

    for red in (
        red_of(xh, y + 2, c), red_of(1 - xh, y + 1, c), red_of(1 - xh, y + 3, c), red_of(1 - xh, y + 2, c),
    ):
        arrived(kv_rows(red), kv_recv.at[red])
        kv_send_to(red, sibling)

    to_sibling(7).wait_recv()
    acc[...] = pp[7, c] + sib[7]
    for k in range(1, 8):
        p = rem(chip + k, 8)
        arrived(qr.at[p], qr_recv.at[p])
        acc[...] += restore(qr.at[p], PROJ)

    def turn(v):
        return (v * cos_ref[...] + pltpu.roll(v, HD // 2, 1) * sin_ref[...]).astype(BF16)

    fresh = pl.ds(pl.multiple_of(CACHE + r * ROWS, ROWS), ROWS)
    kv[fresh, 0:HD] = turn(acc[:, WIDE : WIDE + HD])
    kv[fresh, HD : 2 * HD] = acc[:, WIDE + HD : PROJ].astype(BF16)

    def nk_rows(red):
        return kv.at[pl.ds(pl.multiple_of(CACHE + red * ROWS, ROWS), ROWS), 0 : 2 * HD]

    def nk_to(slot, red, to):
        send(nk_rows(red), nk_rows(red), nk_send.at[slot], nk_recv.at[red], to)

    for k in range(1, 8):
        nk_to(k, r, (b, rem(chip + k, 8) * 2 + c))
    nk_to(0, r, sibling)
    for h in range(8):
        qh[h * ROWS : (h + 1) * ROWS, :] = turn(acc[:, h * HD : (h + 1) * HD])

    for k in range(8):
        red = rem(chip + k, 8) * 2 + 1 - c
        arrived(kv_rows(red), kv_recv.at[red])
    start = start_ref[0]
    turn_log = HD ** (-0.5) * math.log2(math.e)

    def scores(half, n):
        keys = kv[pl.ds(pl.multiple_of(n * CHUNK, CHUNK), CHUNK), 0:HD]
        return lax.dot_general(
            qh[half * HALF : (half + 1) * HALF, :], keys, (((1,), (1,)), ((), ())), preferred_element_type=F32
        )

    def keep(n, t, top):
        s_ref[:, pl.ds(pl.multiple_of(n * CHUNK, CHUNK), CHUNK)] = t
        for k in range(CHUNK // HD):
            top = jnp.maximum(top, t[:, k * HD : (k + 1) * HD])
        return top

    at_count = [0]

    def at_to(half, red, to):
        send(att.at[half, red], att.at[half, red], at_send.at[at_count[0]], at_recv.at[half, red], to)
        at_count[0] += 1

    for half in range(2):
        def plain(n, top, half=half):
            return keep(n, scores(half, n), top)

        def partly(n, top, half=half):
            slot = n * CHUNK + lax.broadcasted_iota(I32, (1, CHUNK), 1)
            return keep(n, scores(half, n) + jnp.where(slot < start, 0.0, NEG), top)

        top = jnp.full((HALF, HD), NEG, F32)
        top = lax.fori_loop(0, 4, plain, top)
        top = lax.fori_loop(4, 8, partly, top)
        if half == 0:
            for k in range(1, 8):
                red = rem(chip + k, 8) * 2 + c
                arrived(nk_rows(red), nk_recv.at[red])
                nk_to(7 + k, red, sibling)
            for k in range(8):
                red = rem(chip + k, 8) * 2 + 1 - c
                arrived(nk_rows(red), nk_recv.at[red])
        token = r * ROWS + rem(lax.broadcasted_iota(I32, (HALF, CHUNK), 0), ROWS)
        ahead = lax.broadcasted_iota(I32, (HALF, CHUNK), 1) > token
        top = keep(8, jnp.where(ahead, NEG, scores(half, 8)), top)
        peak = jnp.broadcast_to(jnp.max(top, axis=1, keepdims=True), (HALF, HD))

        mix[...] = jnp.zeros_like(mix)

        def weigh(n, _):
            base = n * CHUNK
            parts = []
            for k in range(CHUNK // HD):
                t = s_ref[:, pl.ds(pl.multiple_of(base + k * HD, HD), HD)]
                parts.append(jnp.exp2((t - peak) * turn_log).astype(BF16))
            wts = jnp.concatenate(parts, axis=1)
            vals = kv[pl.ds(pl.multiple_of(base, CHUNK), CHUNK), HD : 3 * HD]
            mix[...] += jnp.dot(wts, vals, preferred_element_type=F32)
            return 0

        lax.fori_loop(0, 9, weigh, 0)
        done = (mix[:, 0:HD] / mix[:, HD : 2 * HD]).astype(BF16)
        for h in range(4):
            att[half, r, :, h * HD : (h + 1) * HD] = done[h * ROWS : (h + 1) * ROWS, :]
        for k in range(1, 8):
            at_to(half, r, (b, rem(chip + k, 8) * 2 + c))
        at_to(half, r, sibling)

    for half in range(2):
        for k in range(1, 8):
            red = rem(chip + k, 8) * 2 + c
            arrived(att.at[half, red], at_recv.at[half, red])
            at_to(half, red, sibling)
    for half in range(2):
        for k in range(8):
            red = rem(chip + k, 8) * 2 + 1 - c
            arrived(att.at[half, red], at_recv.at[half, red])

    loads[8].wait()
    own = lambda d: blk_of(xl, z + d)
    other = lambda d: blk_of(ox, z + d)

    def project_out(slots):
        left = jnp.concatenate([att[0, s] for s in slots], axis=0)
        right = jnp.concatenate([att[1, s] for s in slots], axis=0)
        for n in range(WIDE // 256):
            lanes = slice(n * 256, (n + 1) * 256)
            t = jnp.dot(left, wo[0 : WIDE // 2, lanes], preferred_element_type=F32)
            t = t + jnp.dot(right, wo[WIDE // 2 : WIDE, lanes], preferred_element_type=F32)
            for k, s in enumerate(slots):
                op[s, :, lanes] = t[k * ROWS : (k + 1) * ROWS]

    def x_send(k, v):
        quantize(xs.at[k], v)
        send(xs.at[k], xr.at[k], xs_send.at[k], xr_recv.at[k], x_pair)

    def x_get(k):
        arrived(xr.at[k], xr_recv.at[k])
        return restore(xr.at[k], WIDE)

    def z_send(k, v, to):
        quantize(zs.at[k], v)
        send(zs.at[k], zr.at[k], zs_send.at[k], zr_recv.at[k], to)

    def z_get(k):
        arrived(zr.at[k], zr_recv.at[k])
        return restore(zr.at[k], WIDE)

    project_out([other(4), other(-3), other(2), other(-2)])
    x_send(0, op[other(4)])
    z_send(4, op[other(2)], z_up)
    z_send(9, op[other(-2)], z_down)
    x_send(1, op[other(-3)])
    project_out([own(4), own(-3), other(3), own(3)])
    x_send(2, op[other(3)])
    z_send(0, op[own(4)] + x_get(0), z_up)
    z_send(6, op[own(-3)] + x_get(1), z_down)
    project_out([other(1), other(-1), own(2), own(-2)])
    z_send(5, op[other(1)] + z_get(4), z_up)
    z_send(10, op[other(-1)] + z_get(9), z_down)
    project_out([own(1), own(-1), own(0), other(0)])
    z_send(1, op[own(3)] + z_get(0) + x_get(2), z_up)
    z_send(7, op[own(-2)] + z_get(6), z_down)
    x_send(3, op[other(0)] + z_get(5) + z_get(10))
    z_send(2, op[own(2)] + z_get(1), z_up)
    z_send(8, op[own(-1)] + z_get(7), z_down)
    z_send(3, op[own(1)] + z_get(2), z_up)
    out_ref[...] = res[...] + (op[own(0)] + x_get(3) + z_get(8) + z_get(3))

    for cp in sends:
        cp.wait_send()

    def drain(i, _):
        to_sibling(i).wait_send()

        @pl.when(i < 7)
        def _():
            to_chip(i).wait_send()

        return 0

    lax.fori_loop(0, 8, drain, 0)


def on_device(resid, norm_gain, w_query, w_key, w_value, w_out, cache_key, cache_value, prefix_len):
    r = lax.axis_index("red")
    half = HD // 2
    steps = jnp.arange(half, dtype=F32)
    freq = THETA ** (-(steps * 2.0) / HD)
    positions = prefix_len[0] + r * ROWS + jnp.arange(ROWS, dtype=I32)
    angle = positions.astype(F32)[:, None] * freq[None, :]
    cosine, sine = jnp.cos(angle), jnp.sin(angle)
    cosine = jnp.concatenate([cosine, cosine], axis=1)
    sine = jnp.concatenate([-sine, sine], axis=1)
    vmem = pl.BlockSpec(memory_space=pltpu.VMEM)
    hbm = pl.BlockSpec(memory_space=pl.ANY)
    dma = pltpu.SemaphoreType.DMA
    scratch = [
        pltpu.VMEM((ROWS, WIDE), F32),
        pltpu.VMEM((WIDE, PROJ), BF16),
        pltpu.VMEM((WIDE, WIDE), BF16),
        pltpu.VMEM((16, ROWS, WIDE), BF16),
        pltpu.VMEM((KEYS, 3 * HD), BF16),
        pltpu.VMEM((SLOTS, 2 * HD), BF16),
        pltpu.VMEM((16, 8, HD), F32),
        pltpu.VMEM((8, 2, ROWS, PROJ), F32),
        pltpu.VMEM((8, ROWS, PROJ), F32),
        pltpu.VMEM((8, ROWS, PROJ + HD), I16),
        pltpu.VMEM((8, ROWS, PROJ + HD), I16),
        pltpu.VMEM((ROWS, PROJ), F32),
        pltpu.VMEM((8 * ROWS, HD), BF16),
        pltpu.VMEM((HALF, KEYS), F32),
        pltpu.VMEM((HALF, 2 * HD), F32),
        pltpu.VMEM((2, 16, ROWS, WIDE // 2), BF16),
        pltpu.VMEM((16, ROWS, WIDE), F32),
        pltpu.VMEM((4, ROWS, WIDE + HD), I16),
        pltpu.VMEM((4, ROWS, WIDE + HD), I16),
        pltpu.VMEM((11, ROWS, WIDE + HD), I16),
        pltpu.VMEM((11, ROWS, WIDE + HD), I16),
        dma((9,)), dma((16,)), dma((16,)),
        dma((15,)), dma((16,)),
        dma((15,)), dma((16,)),
        dma((8,)), dma((8,)), dma((8,)), dma((8,)),
        dma((15,)), dma((16,)),
        dma((30,)), dma((2, 16)),
        dma((4,)), dma((4,)), dma((11,)), dma((11,)),
    ]
    return pl.pallas_call(
        kernel,
        out_shape=jax.ShapeDtypeStruct((ROWS, WIDE), F32),
        in_specs=[pl.BlockSpec(memory_space=pltpu.SMEM), hbm, vmem, hbm, hbm, hbm, hbm, hbm, hbm, vmem, vmem],
        out_specs=vmem,
        scratch_shapes=scratch,
        compiler_params=pltpu.CompilerParams(
            collective_id=0, has_side_effects=True, vmem_limit_bytes=58 * 1024 * 1024
        ),
    )(prefix_len, resid, norm_gain[None, :], w_query, w_key, w_value, w_out, cache_key, cache_value, cosine, sine)


def solution(mesh):
    placed = (
        P("blk", "red"), P("red"), P("red", "blk"), P("red", None), P("red", None), P("blk", "red"),
        P("red", None), P("red", None), P(),
    )
    return jax.shard_map(on_device, mesh=mesh, in_specs=placed, out_specs=P("blk", "red"), check_vma=False)
```

```python
import functools
import math

import jax
import jax.numpy as jnp
from jax import lax
from jax.experimental import pallas as pl
from jax.experimental.pallas import tpu as pltpu
from jax.sharding import PartitionSpec as P

MESH = pl.DeviceIdType.MESH
F32, BF16, I16, I32 = jnp.float32, jnp.bfloat16, jnp.int16, jnp.int32

HD = 128
THETA = 500000.0
ROWS = 64
WIDE = 1024
PROJ = WIDE + 2 * HD
SLOTS = 512
CACHE = 8192
SPAN = 1024
KEYS = CACHE + SPAN
CHUNK = 1024
PART = 32
HALF = 8 * PART
STEP = 8.0
TOP = 32000.0
NEG = -1e30


def rem(a, n):
    return lax.rem(a, jnp.int32(n))


def quantize(dst, v):
    n = v.shape[1]
    fold = jnp.abs(v[:, :HD])
    for k in range(1, n // HD):
        fold = jnp.maximum(fold, jnp.abs(v[:, k * HD : (k + 1) * HD]))
    top = jnp.max(fold, axis=1, keepdims=True)
    e = jnp.ceil(jnp.log2(jnp.maximum(top, 1e-30)) * STEP)
    e = jnp.broadcast_to(e, (v.shape[0], HD))
    up = jnp.exp2(e * (-1.0 / STEP)) * TOP
    for k in range(n // HD):
        dst[:, k * HD : (k + 1) * HD] = jnp.round(v[:, k * HD : (k + 1) * HD] * up).astype(I32).astype(I16)
    dst[:, n : n + HD] = e.astype(I32).astype(I16)


def restore(src, n):
    e = src[:, n : n + HD].astype(I32).astype(F32)
    down = jnp.exp2(e * (1.0 / STEP)) * (1.0 / TOP)
    return jnp.concatenate(
        [src[:, k * HD : (k + 1) * HD].astype(I32).astype(F32) * down for k in range(n // HD)], axis=1
    )


def kernel(
    start_ref, resid_hbm, gain_ref, wq_hbm, wk_hbm, wv_hbm, wo_hbm, ck_hbm, cv_hbm, cos_ref, sin_ref,
    out_ref,
    res, w, wo, g, gs, kv, pb, sq, pp, ks, kr, qs, qr, qh, s_ref, mix, att, op, xs, xr, zs, zr,
    load_sem, w_sem, sq_send, sq_recv, ag_send, ag_recv, gs_send, gs_recv, kv_send, kv_recv,
    ks_send, kr_recv, qs_send, qr_recv, nk_send, nk_recv, at_send, at_recv, xs_send, xr_recv, zs_send, zr_recv,
):
    b = lax.axis_index("blk")
    r = lax.axis_index("red")
    xl, z = lax.div(b, jnp.int32(8)), rem(b, 8)
    xh, y, c = lax.div(r, jnp.int32(8)), rem(lax.div(r, jnp.int32(2)), 4), rem(r, 2)
    chip = lax.div(r, jnp.int32(2))
    head = lax.div(b, jnp.int32(2))
    ox = 1 - xl

    def blk_of(px, pz):
        return px * 8 + rem(pz + 16, 8)

    def red_of(px, py, pc):
        return (px * 4 + rem(py + 8, 4)) * 2 + pc

    z_next = {1: (blk_of(xl, z + 1), r), -1: (blk_of(xl, z - 1), r)}
    x_pair = (blk_of(ox, z), r)
    x_across = (blk_of(ox, z), red_of(1 - xh, y, c))
    sibling = (b, red_of(xh, y, 1 - c))
    others = []
    for dx, dy in ((1, 2), (0, 1), (1, 0), (0, 3), (1, 1), (0, 2), (1, 3)):
        p = lax.div(red_of(rem(xh + dx, 2), y + dy, 0), jnp.int32(2))
        others.append((p, (b, p * 2 + c)))

    barrier = pltpu.get_barrier_semaphore()
    peers = [(b, rem(r + i, 16)) for i in range(1, 16)] + [z_next[1], z_next[-1], x_pair, x_across]
    for p in peers:
        pl.semaphore_signal(barrier, inc=1, device_id=p, device_id_type=MESH)

    mine = pl.ds(pl.multiple_of(r * SLOTS, SLOTS), SLOTS)
    my_cols = pl.ds(pl.multiple_of(head * HD, HD), HD)
    pair_head = lax.div(blk_of(ox, z), jnp.int32(2))
    pair_cols = pl.ds(pl.multiple_of(pair_head * HD, HD), HD)
    loads = [
        pltpu.make_async_copy(resid_hbm, res, load_sem.at[0]),
        pltpu.make_async_copy(ck_hbm.at[:, my_cols], kv.at[mine, 0:HD], load_sem.at[1]),
        pltpu.make_async_copy(cv_hbm.at[:, my_cols], kv.at[mine, HD : 2 * HD], load_sem.at[2]),
        pltpu.make_async_copy(ck_hbm.at[:, pair_cols], pb.at[:, 0:HD], load_sem.at[3]),
        pltpu.make_async_copy(cv_hbm.at[:, pair_cols], pb.at[:, HD : 2 * HD], load_sem.at[4]),
        pltpu.make_async_copy(wq_hbm, w.at[0, :, 0:WIDE], load_sem.at[5]),
        pltpu.make_async_copy(wk_hbm.at[:, my_cols], w.at[0, :, WIDE : WIDE + HD], load_sem.at[6]),
        pltpu.make_async_copy(wv_hbm.at[:, my_cols], w.at[0, :, WIDE + HD : PROJ], load_sem.at[7]),
        pltpu.make_async_copy(wo_hbm, wo, load_sem.at[8]),
    ]
    for cp in loads:
        cp.start()

    sends = []

    def send(src, dst, ssem, rsem, to):
        cp = pltpu.make_async_remote_copy(
            src_ref=src, dst_ref=dst, send_sem=ssem, recv_sem=rsem, device_id=to, device_id_type=MESH
        )
        cp.start()
        sends.append(cp)

    def arrived(dst, rsem):
        pltpu.make_async_remote_copy(
            src_ref=dst, dst_ref=dst, send_sem=load_sem.at[0], recv_sem=rsem, device_id=sibling, device_id_type=MESH
        ).wait_recv()

    loads[0].wait()
    fold = jnp.zeros((ROWS, HD), F32)
    for k in range(WIDE // HD):
        v = res[:, k * HD : (k + 1) * HD]
        fold = fold + v * v
    square = jnp.concatenate([fold, jnp.zeros((HD - ROWS, HD), F32)], axis=0).T
    sq[r] = jnp.broadcast_to(jnp.sum(square, axis=0, keepdims=True), (8, HD))
    pl.semaphore_wait(barrier, len(peers))
    for i, (p, to) in enumerate(others):
        send(sq.at[r], sq.at[r], sq_send.at[2 * i], sq_recv.at[r], to)
        send(sq.at[r], sq.at[r], sq_send.at[2 * i + 1], sq_recv.at[r], (b, p * 2 + 1 - c))
    send(sq.at[r], sq.at[r], sq_send.at[14], sq_recv.at[r], sibling)

    for cp in loads[1:5]:
        cp.wait()

    def kv_rows(red):
        return kv.at[pl.ds(pl.multiple_of(red * SLOTS, SLOTS), SLOTS), 0 : 2 * HD]

    kv_count = [0]

    def kv_send_to(red, to, src=None):
        send(kv_rows(red) if src is None else src, kv_rows(red), kv_send.at[kv_count[0]], kv_recv.at[red], to)
        kv_count[0] += 1

    kv_send_to(r, x_across, src=pb)
    for d in (1, 3, 2):
        kv_send_to(r, (b, red_of(xh, y + d, c)))

    kv[:, 2 * HD : 3 * HD] = jnp.ones((KEYS, HD), BF16)

    for i in range(1, 16):
        p = rem(r + i, 16)
        arrived(sq.at[p], sq_recv.at[p])
    total = jnp.sum(sq[...], axis=0)[0:1]
    column = jnp.broadcast_to(total, (HD, HD)).T[:ROWS]
    factor = lax.rsqrt(column / (WIDE * 16.0) + 1e-05)
    gain = gain_ref[...]

    def g_at(h, px, pz):
        pz = rem(pz + 16, 8)
        return g.at[h, rem(pz, 2), px * 4 + lax.div(pz, jnp.int32(2))]

    ag_count = [0, 0]

    def g_wait(h, px, d):
        pz = z + (1 - 2 * h) * d
        arrived(g_at(h, px, pz), ag_recv.at[h, blk_of(px, pz)])

    def g_send(h, px, d, *to):
        pz = z + (1 - 2 * h) * d
        for t in to:
            device = x_pair if t == 0 else z_next[t * (1 - 2 * h)]
            send(g_at(h, px, pz), g_at(h, px, pz), ag_send.at[h, ag_count[h]], ag_recv.at[h, blk_of(px, pz)], device)
            ag_count[h] += 1

    gs_count = [0, 0]

    def g_trade(h, px, d, e):
        s = 1 - 2 * h
        pz = rem(z + 16 + jnp.where(rem(z + 16 + s * d, 2) == 1 - c, s * d, s * e), 8)
        j = px * 4 + lax.div(pz, jnp.int32(2))
        send(g.at[h, 1 - c, j], gs.at[h, j], gs_send.at[h, gs_count[h]], gs_recv.at[h, j], sibling)
        gs_count[h] += 1

    def gather(h, stage):
        if stage == 0:
            rows = slice(h * PART, (h + 1) * PART)
            slot = g_at(h, xl, z)
            for k in range(WIDE // HD):
                lanes = slice(k * HD, (k + 1) * HD)
                slot[:, lanes] = (res[rows, lanes] * factor[rows] * gain[:, lanes]).astype(BF16)
            g_send(h, xl, 0, 1, -1, 0)
        if stage == 1:
            g_wait(h, xl, -1)
            g_send(h, xl, -1, 1)
            g_wait(h, xl, 1)
            g_send(h, xl, 1, -1)
            g_wait(h, ox, 0)
            g_send(h, ox, 0, 1, -1)
            g_trade(h, xl, 0, -1)
        if stage == 2:
            g_wait(h, xl, -2)
            g_send(h, xl, -2, 1)
            g_wait(h, xl, 2)
            g_send(h, xl, 2, -1)
            g_wait(h, ox, -1)
            g_send(h, ox, -1, 1)
            g_wait(h, ox, 1)
            g_send(h, ox, 1, -1)
            g_trade(h, xl, 1, -2)
            g_trade(h, ox, 0, -1)
        if stage == 3:
            g_wait(h, xl, -3)
            g_send(h, xl, -3, 1, 0)
            g_wait(h, xl, 3)
            g_send(h, xl, 3, 0)
            g_trade(h, xl, 2, -3)
        if stage == 4:
            g_wait(h, xl, -4)
            g_send(h, xl, -4, 0)
            g_trade(h, xl, 3, -4)
        if stage == 5:
            g_wait(h, ox, -2)
            g_wait(h, ox, 2)
            g_trade(h, ox, 1, -2)
            g_wait(h, ox, -3)
            g_wait(h, ox, 3)
            g_trade(h, ox, 2, -3)
        if stage == 6:
            g_wait(h, ox, -4)
            g_trade(h, ox, 3, -4)
            for j in range(8):
                arrived(gs.at[h, j], gs_recv.at[h, j])

    def project(h):
        x0 = g.at[h, c][...].reshape(8 * PART, WIDE)
        x1 = gs[h].reshape(8 * PART, WIDE)

        def columns(n):
            lanes = slice(n * 256, (n + 1) * 256)
            t = jnp.dot(x0, w[0, :, lanes], preferred_element_type=F32)
            t = t + jnp.dot(x1, w[1, :, lanes], preferred_element_type=F32)
            pp[h, :, :, lanes] = t.reshape(8, PART, 256)

        columns(WIDE // 256)
        for i, (p, to) in enumerate(others):
            quantize(ks.at[h, i], pp[h, p, :, WIDE:PROJ])
            send(ks.at[h, i], kr.at[h, chip], ks_send.at[h, i], kr_recv.at[h, chip], to)
        for n in range(WIDE // 256):
            columns(n)
        for i, (p, to) in enumerate(others):
            quantize(qs.at[h, i], pp[h, p, :, 0:WIDE])
            send(qs.at[h, i], qr.at[h, chip], qs_send.at[h, i], qr_recv.at[h, chip], to)

    gather(0, 0)
    gather(1, 0)
    send(kv_rows(r), kv_rows(r), kv_send.at[kv_count[0]], kv_recv.at[r], sibling)
    kv_count[0] += 1
    for cp in loads[5:8]:
        cp.wait()
    send(w.at[0], w.at[1], w_sem.at[0], w_sem.at[1], sibling)
    gather(0, 1)
    gather(1, 1)
    r_across = red_of(1 - xh, y, c)
    arrived(kv_rows(r_across), kv_recv.at[r_across])
    for d in (1, 3, 2):
        kv_send_to(r_across, (b, red_of(xh, y + d, c)))
    gather(0, 2)
    gather(1, 2)
    kv_send_to(r_across, sibling)
    gather(0, 3)
    gather(1, 3)
    gather(0, 4)
    gather(0, 5)
    gather(1, 4)
    gather(0, 6)
    arrived(w.at[1], w_sem.at[1])
    project(0)
    gather(1, 5)
    gather(1, 6)
    project(1)

    for red in (
        red_of(xh, y + 1, c), red_of(xh, y + 3, c), red_of(xh, y + 2, c),
        red_of(1 - xh, y + 1, c), red_of(1 - xh, y + 3, c), red_of(1 - xh, y + 2, c),
    ):
        arrived(kv_rows(red), kv_recv.at[red])
        kv_send_to(red, sibling)

    def turn(h, v):
        rows = slice(h * PART, (h + 1) * PART)
        return (v * cos_ref[rows] + pltpu.roll(v, HD // 2, 1) * sin_ref[rows]).astype(BF16)

    for h in range(2):
        new = pp[h, chip, :, WIDE:PROJ]
        for p, _ in others:
            arrived(kr.at[h, p], kr_recv.at[h, p])
            new = new + restore(kr.at[h, p], 2 * HD)
        fresh = pl.ds(pl.multiple_of(CACHE + r * ROWS + h * PART, PART), PART)
        kv[fresh, 0:HD] = turn(h, new[:, 0:HD])
        kv[fresh, HD : 2 * HD] = new[:, HD : 2 * HD].astype(BF16)

    def nk_rows(red):
        return kv.at[pl.ds(pl.multiple_of(CACHE + red * ROWS, ROWS), ROWS), 0 : 2 * HD]

    def nk_to(slot, red, to):
        send(nk_rows(red), nk_rows(red), nk_send.at[slot], nk_recv.at[red], to)

    for i, (p, to) in enumerate(others):
        nk_to(i, r, to)
    nk_to(7, r, sibling)

    for k in range(8):
        red = rem(chip + k, 8) * 2 + 1 - c
        arrived(kv_rows(red), kv_recv.at[red])
    start = start_ref[0]
    turn_log = HD ** (-0.5) * math.log2(math.e)

    def scores(h, n):
        keys = kv[pl.ds(pl.multiple_of(n * CHUNK, CHUNK), CHUNK), 0:HD]
        return lax.dot_general(qh[h], keys, (((1,), (1,)), ((), ())), preferred_element_type=F32)

    def keep(h, n, t, top):
        s_ref[h, :, pl.ds(pl.multiple_of(n * CHUNK, CHUNK), CHUNK)] = t
        for k in range(CHUNK // HD):
            top = jnp.maximum(top, t[:, k * HD : (k + 1) * HD])
        return top

    tops = []
    for h in range(2):
        query = pp[h, chip, :, 0:WIDE]
        for p, _ in others:
            arrived(qr.at[h, p], qr_recv.at[h, p])
            query = query + restore(qr.at[h, p], WIDE)
        for k in range(8):
            qh[h, k * PART : (k + 1) * PART, :] = turn(h, query[:, k * HD : (k + 1) * HD])

        def plain(n, top, h=h):
            return keep(h, n, scores(h, n), top)

        def partly(n, top, h=h):
            slot = n * CHUNK + lax.broadcasted_iota(I32, (1, CHUNK), 1)
            return keep(h, n, scores(h, n) + jnp.where(slot < start, 0.0, NEG), top)

        top = jnp.full((HALF, HD), NEG, F32)
        top = lax.fori_loop(0, 4, plain, top)
        tops.append(lax.fori_loop(4, 8, partly, top))

    for i, (p, _) in enumerate(others):
        red = p * 2 + c
        arrived(nk_rows(red), nk_recv.at[red])
        nk_to(8 + i, red, sibling)
    for k in range(8):
        red = rem(chip + k, 8) * 2 + 1 - c
        arrived(nk_rows(red), nk_recv.at[red])

    at_count = [0, 0]

    def at_to(h, red, to):
        send(att.at[h, red], att.at[h, red], at_send.at[h, at_count[h]], at_recv.at[h, red], to)
        at_count[h] += 1

    for h in range(2):
        token = r * ROWS + h * PART + rem(lax.broadcasted_iota(I32, (HALF, CHUNK), 0), PART)
        ahead = lax.broadcasted_iota(I32, (HALF, CHUNK), 1) > token
        top = keep(h, 8, jnp.where(ahead, NEG, scores(h, 8)), tops[h])
        peak = jnp.broadcast_to(jnp.max(top, axis=1, keepdims=True), (HALF, HD))

        mix[...] = jnp.zeros_like(mix)

        def weigh(n, _, h=h, peak=peak):
            base = n * CHUNK
            parts = []
            for k in range(CHUNK // HD):
                t = s_ref[h, :, pl.ds(pl.multiple_of(base + k * HD, HD), HD)]
                parts.append(jnp.exp2((t - peak) * turn_log).astype(BF16))
            wts = jnp.concatenate(parts, axis=1)
            vals = kv[pl.ds(pl.multiple_of(base, CHUNK), CHUNK), HD : 3 * HD]
            mix[...] += jnp.dot(wts, vals, preferred_element_type=F32)
            return 0

        lax.fori_loop(0, 9, weigh, 0)
        done = (mix[:, 0:HD] / mix[:, HD : 2 * HD]).astype(BF16)
        for k in range(8):
            att[h, r, :, k * HD : (k + 1) * HD] = done[k * PART : (k + 1) * PART, :]
        for p, to in others:
            at_to(h, r, to)
        at_to(h, r, sibling)

    loads[8].wait()

    def project_out(h):
        for p, _ in others:
            red = p * 2 + c
            arrived(att.at[h, red], at_recv.at[h, red])
            at_to(h, red, sibling)
        for k in range(8):
            red = rem(chip + k, 8) * 2 + 1 - c
            arrived(att.at[h, red], at_recv.at[h, red])
        for m in range(2):
            x = att[h, m * 8 : (m + 1) * 8].reshape(8 * PART, WIDE)
            for n in range(WIDE // 256):
                lanes = slice(n * 256, (n + 1) * 256)
                t = jnp.dot(x, wo[:, lanes], preferred_element_type=F32)
                op[h, m * 8 : (m + 1) * 8, :, lanes] = t.reshape(8, PART, 256)

    def ring(h, stage):
        s = 1 - 2 * h
        up, down = z_next[s], z_next[-s]

        def own(d):
            return op[h, blk_of(xl, z + s * d)]

        def other(d):
            return op[h, blk_of(ox, z + s * d)]

        def x_send(k, v):
            quantize(xs.at[h, k], v)
            send(xs.at[h, k], xr.at[h, k], xs_send.at[h, k], xr_recv.at[h, k], x_pair)

        def x_get(k):
            arrived(xr.at[h, k], xr_recv.at[h, k])
            return restore(xr.at[h, k], WIDE)

        def z_send(k, v, to):
            quantize(zs.at[h, k], v)
            send(zs.at[h, k], zr.at[h, k], zs_send.at[h, k], zr_recv.at[h, k], to)

        def z_get(k):
            arrived(zr.at[h, k], zr_recv.at[h, k])
            return restore(zr.at[h, k], WIDE)

        if stage == 0:
            x_send(0, other(4))
            z_send(4, other(2), up)
            z_send(9, other(-2), down)
            x_send(1, other(-3))
            x_send(2, other(3))
        if stage == 1:
            z_send(0, own(4) + x_get(0), up)
            z_send(6, own(-3) + x_get(1), down)
        if stage == 2:
            z_send(5, other(1) + z_get(4), up)
            z_send(10, other(-1) + z_get(9), down)
        if stage == 3:
            z_send(1, own(3) + z_get(0) + x_get(2), up)
            z_send(7, own(-2) + z_get(6), down)
        if stage == 4:
            x_send(3, other(0) + z_get(5) + z_get(10))
        if stage == 5:
            z_send(2, own(2) + z_get(1), up)
            z_send(8, own(-1) + z_get(7), down)
        if stage == 6:
            z_send(3, own(1) + z_get(2), up)
        if stage == 7:
            rows = slice(h * PART, (h + 1) * PART)
            out_ref[rows] = res[rows] + (own(0) + x_get(3) + z_get(8) + z_get(3))

    project_out(0)
    ring(0, 0)
    ring(0, 1)
    ring(0, 2)
    project_out(1)
    ring(1, 0)
    ring(0, 3)
    ring(1, 1)
    ring(1, 2)
    ring(0, 4)
    ring(0, 5)
    ring(1, 3)
    ring(0, 6)
    ring(1, 4)
    ring(1, 5)
    ring(0, 7)
    ring(1, 6)
    ring(1, 7)

    for cp in sends:
        cp.wait_send()


def on_device(resid, norm_gain, w_query, w_key, w_value, w_out, cache_key, cache_value, prefix_len):
    r = lax.axis_index("red")
    half = HD // 2
    steps = jnp.arange(half, dtype=F32)
    freq = THETA ** (-(steps * 2.0) / HD)
    positions = prefix_len[0] + r * ROWS + jnp.arange(ROWS, dtype=I32)
    angle = positions.astype(F32)[:, None] * freq[None, :]
    cosine, sine = jnp.cos(angle), jnp.sin(angle)
    cosine = jnp.concatenate([cosine, cosine], axis=1)
    sine = jnp.concatenate([-sine, sine], axis=1)
    vmem = pl.BlockSpec(memory_space=pltpu.VMEM)
    hbm = pl.BlockSpec(memory_space=pl.ANY)
    dma = pltpu.SemaphoreType.DMA
    scratch = [
        pltpu.VMEM((ROWS, WIDE), F32),
        pltpu.VMEM((2, WIDE, PROJ), BF16),
        pltpu.VMEM((WIDE, WIDE), BF16),
        pltpu.VMEM((2, 2, 8, PART, WIDE), BF16),
        pltpu.VMEM((2, 8, PART, WIDE), BF16),
        pltpu.VMEM((KEYS, 3 * HD), BF16),
        pltpu.VMEM((SLOTS, 2 * HD), BF16),
        pltpu.VMEM((16, 8, HD), F32),
        pltpu.VMEM((2, 8, PART, PROJ), F32),
        pltpu.VMEM((2, 7, PART, 3 * HD), I16),
        pltpu.VMEM((2, 8, PART, 3 * HD), I16),
        pltpu.VMEM((2, 7, PART, WIDE + HD), I16),
        pltpu.VMEM((2, 8, PART, WIDE + HD), I16),
        pltpu.VMEM((2, 8 * PART, HD), BF16),
        pltpu.VMEM((2, HALF, KEYS), F32),
        pltpu.VMEM((HALF, 2 * HD), F32),
        pltpu.VMEM((2, 16, PART, WIDE), BF16),
        pltpu.VMEM((2, 16, PART, WIDE), F32),
        pltpu.VMEM((2, 4, PART, WIDE + HD), I16),
        pltpu.VMEM((2, 4, PART, WIDE + HD), I16),
        pltpu.VMEM((2, 11, PART, WIDE + HD), I16),
        pltpu.VMEM((2, 11, PART, WIDE + HD), I16),
        dma((9,)), dma((2,)), dma((15,)), dma((16,)),
        dma((2, 15)), dma((2, 16)), dma((2, 8)), dma((2, 8)),
        dma((15,)), dma((16,)),
        dma((2, 7)), dma((2, 8)), dma((2, 7)), dma((2, 8)),
        dma((15,)), dma((16,)),
        dma((2, 15)), dma((2, 16)),
        dma((2, 4)), dma((2, 4)), dma((2, 11)), dma((2, 11)),
    ]
    return pl.pallas_call(
        kernel,
        out_shape=jax.ShapeDtypeStruct((ROWS, WIDE), F32),
        in_specs=[pl.BlockSpec(memory_space=pltpu.SMEM), hbm, vmem, hbm, hbm, hbm, hbm, hbm, hbm, vmem, vmem],
        out_specs=vmem,
        scratch_shapes=scratch,
        compiler_params=pltpu.CompilerParams(
            collective_id=0, has_side_effects=True, vmem_limit_bytes=58 * 1024 * 1024
        ),
    )(prefix_len, resid, norm_gain[None, :], w_query, w_key, w_value, w_out, cache_key, cache_value, cosine, sine)


def solution(mesh):
    placed = (
        P("blk", "red"), P("red"), P("red", "blk"), P("red", None), P("red", None), P("blk", "red"),
        P("red", None), P("red", None), P(),
    )
    return jax.shard_map(on_device, mesh=mesh, in_specs=placed, out_specs=P("blk", "red"), check_vma=False)
```

```python
import functools
import math

import jax
import jax.numpy as jnp
from jax import lax
from jax.experimental import pallas as pl
from jax.experimental.pallas import tpu as pltpu
from jax.sharding import PartitionSpec as P

MESH = pl.DeviceIdType.MESH
F32, BF16, I16, I32 = jnp.float32, jnp.bfloat16, jnp.int16, jnp.int32

HD = 128
THETA = 500000.0
ROWS = 64
WIDE = 1024
PROJ = WIDE + 2 * HD
SLOTS = 512
CACHE = 8192
SPAN = 1024
KEYS = CACHE + SPAN
CHUNK = 1024
PIECES = ((0, 32), (32, 32))
EARLY = 4
LANES = 32
STEP = 8.0
TOP = 32000.0
NEG = -1e30


def rem(a, n):
    return lax.rem(a, jnp.int32(n))


def tiles(rows, lanes):
    return rows // 16 * (lanes // HD) + 1


def quantize(dst, v):
    wide, groups = v.shape[1] // HD, v.shape[0] // 16
    lane = lax.broadcasted_iota(I32, (16, HD), 1)
    exponents = jnp.zeros((16, HD), F32)
    for m in range(groups):
        rows = v[m * 16 : (m + 1) * 16]
        fold = jnp.abs(rows[:, :HD])
        for k in range(1, wide):
            fold = jnp.maximum(fold, jnp.abs(rows[:, k * HD : (k + 1) * HD]))
        top = jnp.max(fold, axis=1, keepdims=True)
        e = jnp.broadcast_to(jnp.ceil(jnp.log2(jnp.maximum(top, 1e-30)) * STEP), (16, HD))
        exponents = e if m == 0 else jnp.where(lane < m * LANES, exponents, e)
        up = jnp.exp2(e * (-1.0 / STEP)) * TOP
        for k in range(wide):
            dst[m * wide + k] = jnp.round(rows[:, k * HD : (k + 1) * HD] * up).astype(I32).astype(I16)
    dst[groups * wide] = exponents.astype(I32).astype(I16)


def restore(src, groups, wide):
    e = src[groups * wide].astype(I32).astype(F32)
    parts = []
    for m in range(groups):
        lane = m * LANES
        down = jnp.broadcast_to(jnp.exp2(e[:, lane : lane + 1] * (1.0 / STEP)) * (1.0 / TOP), (16, HD))
        parts.append(
            jnp.concatenate([src[m * wide + k].astype(I32).astype(F32) * down for k in range(wide)], axis=1)
        )
    return jnp.concatenate(parts, axis=0)


def kernel(
    start_ref, resid_hbm, gain_ref, wq_hbm, wk_hbm, wv_hbm, wo_hbm, ck_hbm, cv_hbm, freq_ref,
    out_ref,
    cos_ref, sin_ref, res, w, wo, kv, pb, sq,
    load_sem, w_sem, sq_send, sq_recv, kv_send, kv_recv, nk_send, nk_recv,
    *per_piece,
):
    (
        g, gs, pp, ks, kr, qs, qr, qh, s_ref, mix,
        att, op, xs, xr, zs, zr,
        ag_send, ag_recv, gs_send, gs_recv, ks_send, kr_recv, qs_send, qr_recv,
        at_send, at_recv, xs_send, xr_recv, zs_send, zr_recv,
    ) = [per_piece[k :: 30] for k in range(30)]
    count = len(PIECES)
    sense = [1 - 2 * (h % 2) for h in range(count)]
    extent = [slice(first, first + rows) for first, rows in PIECES]
    size = [rows for _, rows in PIECES]
    b = lax.axis_index("blk")
    r = lax.axis_index("red")
    xl, z = lax.div(b, jnp.int32(8)), rem(b, 8)
    xh, y, c = lax.div(r, jnp.int32(8)), rem(lax.div(r, jnp.int32(2)), 4), rem(r, 2)
    chip = lax.div(r, jnp.int32(2))
    head = lax.div(b, jnp.int32(2))
    ox = 1 - xl

    def blk_of(px, pz):
        return px * 8 + rem(pz + 16, 8)

    def red_of(px, py, pc):
        return (px * 4 + rem(py + 8, 4)) * 2 + pc

    z_next = {1: (blk_of(xl, z + 1), r), -1: (blk_of(xl, z - 1), r)}
    z_over = {1: (blk_of(xl, z + 2), r), -1: (blk_of(xl, z - 2), r)}
    x_pair = (blk_of(ox, z), r)
    x_across = (blk_of(ox, z), red_of(1 - xh, y, c))
    sibling = (b, red_of(xh, y, 1 - c))
    others = []
    for dx, dy in ((1, 2), (0, 1), (1, 0), (0, 3), (1, 1), (0, 2), (1, 3)):
        p = lax.div(red_of(rem(xh + dx, 2), y + dy, 0), jnp.int32(2))
        others.append((p, (b, p * 2 + c)))

    nearest = [others[i] for i in (1, 3, 2, 5, 4, 6, 0)]

    barrier = pltpu.get_barrier_semaphore()
    peers = [(b, rem(r + i, 16)) for i in range(1, 16)] + [z_next[1], z_next[-1], z_over[1], z_over[-1], x_pair, x_across]
    for p in peers:
        pl.semaphore_signal(barrier, inc=1, device_id=p, device_id_type=MESH)

    mine = pl.ds(pl.multiple_of(r * SLOTS, SLOTS), SLOTS)
    my_cols = pl.ds(pl.multiple_of(head * HD, HD), HD)
    pair_head = lax.div(blk_of(ox, z), jnp.int32(2))
    pair_cols = pl.ds(pl.multiple_of(pair_head * HD, HD), HD)
    loads = [
        pltpu.make_async_copy(resid_hbm, res, load_sem.at[0]),
        pltpu.make_async_copy(ck_hbm.at[:, my_cols], kv.at[mine, 0:HD], load_sem.at[1]),
        pltpu.make_async_copy(cv_hbm.at[:, my_cols], kv.at[mine, HD : 2 * HD], load_sem.at[2]),
        pltpu.make_async_copy(ck_hbm.at[:, pair_cols], pb.at[:, 0:HD], load_sem.at[3]),
        pltpu.make_async_copy(cv_hbm.at[:, pair_cols], pb.at[:, HD : 2 * HD], load_sem.at[4]),
        pltpu.make_async_copy(wq_hbm, w.at[0, :, 0:WIDE], load_sem.at[5]),
        pltpu.make_async_copy(wk_hbm.at[:, my_cols], w.at[0, :, WIDE : WIDE + HD], load_sem.at[6]),
        pltpu.make_async_copy(wv_hbm.at[:, my_cols], w.at[0, :, WIDE + HD : PROJ], load_sem.at[7]),
        pltpu.make_async_copy(wo_hbm, wo, load_sem.at[8]),
    ]
    for cp in loads:
        cp.start()

    sends = []

    def send(src, dst, ssem, rsem, to):
        cp = pltpu.make_async_remote_copy(
            src_ref=src, dst_ref=dst, send_sem=ssem, recv_sem=rsem, device_id=to, device_id_type=MESH
        )
        cp.start()
        sends.append(cp)

    def sent(keep):
        for cp in sends[: len(sends) - len(keep)]:
            cp.wait_send()
        sends[:] = list(keep)

    def arrived(dst, rsem):
        pltpu.make_async_remote_copy(
            src_ref=dst, dst_ref=dst, send_sem=load_sem.at[0], recv_sem=rsem, device_id=sibling, device_id_type=MESH
        ).wait_recv()

    kv[:, 2 * HD : 3 * HD] = jnp.ones((KEYS, HD), BF16)

    start = start_ref[0]
    position = (start + r * ROWS + lax.broadcasted_iota(I32, (ROWS, HD), 0)).astype(F32)
    angle = position * freq_ref[...]
    first = lax.broadcasted_iota(I32, (ROWS, HD), 1) < HD // 2
    cos_ref[...] = jnp.cos(angle)
    sine = jnp.sin(angle)
    sin_ref[...] = jnp.where(first, -sine, sine)

    loads[0].wait()
    fold = jnp.zeros((ROWS, HD), F32)
    for k in range(WIDE // HD):
        v = res[:, k * HD : (k + 1) * HD]
        fold = fold + v * v
    square = jnp.concatenate([fold, jnp.zeros((HD - ROWS, HD), F32)], axis=0).T
    sq[r] = jnp.broadcast_to(jnp.sum(square, axis=0, keepdims=True), (8, HD))
    pl.semaphore_wait(barrier, len(peers))
    for i, (p, to) in enumerate(others):
        send(sq.at[r], sq.at[r], sq_send.at[2 * i], sq_recv.at[r], to)
        send(sq.at[r], sq.at[r], sq_send.at[2 * i + 1], sq_recv.at[r], (b, p * 2 + 1 - c))
    send(sq.at[r], sq.at[r], sq_send.at[14], sq_recv.at[r], sibling)

    for cp in loads[1:5]:
        cp.wait()

    def kv_rows(red):
        return kv.at[pl.ds(pl.multiple_of(red * SLOTS, SLOTS), SLOTS), 0 : 2 * HD]

    kv_count = [0]

    def kv_send_to(red, to, src=None):
        send(kv_rows(red) if src is None else src, kv_rows(red), kv_send.at[kv_count[0]], kv_recv.at[red], to)
        kv_count[0] += 1

    kv_send_to(r, x_across, src=pb)
    for d in (1, 3, 2):
        kv_send_to(r, (b, red_of(xh, y + d, c)))

    for i in range(1, 16):
        p = rem(r + i, 16)
        arrived(sq.at[p], sq_recv.at[p])
    total = jnp.sum(sq[...], axis=0)[0:1]
    column = jnp.broadcast_to(total, (HD, HD)).T[:ROWS]
    factor = lax.rsqrt(column / (WIDE * 16.0) + 1e-05)
    gain = gain_ref[...]

    def g_at(h, px, pz):
        pz = rem(pz + 16, 8)
        return g[h].at[rem(pz, 2), px * 4 + lax.div(pz, jnp.int32(2))]

    ag_count = [0] * count

    def g_wait(h, px, d):
        pz = z + sense[h] * d
        arrived(g_at(h, px, pz), ag_recv[h].at[blk_of(px, pz)])

    def g_send(h, px, d, *to):
        pz = z + sense[h] * d
        for t in to:
            s = sense[h] * t
            device = {0: x_pair, 1: z_next.get(s), 2: z_over.get(s // 2)}[abs(t)]
            send(g_at(h, px, pz), g_at(h, px, pz), ag_send[h].at[ag_count[h]], ag_recv[h].at[blk_of(px, pz)], device)
            ag_count[h] += 1

    gs_count = [0] * count

    def g_trade(h, px, d, e):
        s = sense[h]
        pz = rem(z + 16 + jnp.where(rem(z + 16 + s * d, 2) == 1 - c, s * d, s * e), 8)
        j = px * 4 + lax.div(pz, jnp.int32(2))
        send(g[h].at[1 - c, j], gs[h].at[j], gs_send[h].at[gs_count[h]], gs_recv[h].at[j], sibling)
        gs_count[h] += 1

    def gather(h, stage):
        if stage == 0:
            rows = extent[h]
            slot = g_at(h, xl, z)
            for k in range(WIDE // HD):
                lanes = slice(k * HD, (k + 1) * HD)
                slot[:, lanes] = (res[rows, lanes] * factor[rows] * gain[:, lanes]).astype(BF16)
            g_send(h, xl, 0, 1, -1, 0)
        if stage == 1:
            g_wait(h, xl, -1)
            g_send(h, xl, -1, 1)
            g_wait(h, xl, 1)
            g_send(h, xl, 1, -1)
            g_wait(h, ox, 0)
            g_send(h, ox, 0, 1, -1)
            g_trade(h, xl, 0, -1)
        if stage == 2:
            g_wait(h, xl, -2)
            g_send(h, xl, -2, 1)
            g_wait(h, xl, 2)
            g_send(h, xl, 2, -1)
            g_wait(h, ox, -1)
            g_send(h, ox, -1, 1)
            g_wait(h, ox, 1)
            g_send(h, ox, 1, -1)
            g_trade(h, xl, 1, -2)
            g_trade(h, ox, 0, -1)
        if stage == 3:
            g_wait(h, xl, -3)
            g_send(h, xl, -3, 1, 0)
            g_wait(h, xl, 3)
            g_send(h, xl, 3, 0)
            g_trade(h, xl, 2, -3)
        if stage == 4:
            g_wait(h, xl, -4)
            g_send(h, xl, -4, 0)
            g_trade(h, xl, 3, -4)
        if stage == 5:
            g_wait(h, ox, -2)
            g_wait(h, ox, 2)
            g_trade(h, ox, 1, -2)
            g_wait(h, ox, -3)
            g_wait(h, ox, 3)
            g_trade(h, ox, 2, -3)
        if stage == 6:
            g_wait(h, ox, -4)
            g_trade(h, ox, 3, -4)
            for j in range(8):
                arrived(gs[h].at[j], gs_recv[h].at[j])

    def project(h):
        x0 = g[h].at[c][...].reshape(8 * size[h], WIDE)
        x1 = gs[h][...].reshape(8 * size[h], WIDE)

        def columns(n):
            lanes = slice(n * 256, (n + 1) * 256)
            t = jnp.dot(x0, w[0, :, lanes], preferred_element_type=F32)
            t = t + jnp.dot(x1, w[1, :, lanes], preferred_element_type=F32)
            pp[h][:, :, lanes] = t.reshape(8, size[h], 256)

        columns(WIDE // 256)
        for i, (p, to) in enumerate(others):
            quantize(ks[h].at[i], pp[h][p, :, WIDE:PROJ])
            send(ks[h].at[i], kr[h].at[chip], ks_send[h].at[i], kr_recv[h].at[chip], to)
        for n in range(WIDE // 256):
            columns(n)

    def send_queries(h, which):
        for i in which:
            p, to = others[i]
            quantize(qs[h].at[i], pp[h][p, :, 0:WIDE])
            send(qs[h].at[i], qr[h].at[chip], qs_send[h].at[i], qr_recv[h].at[chip], to)

    for h in range(count):
        gather(h, 0)
    send(kv_rows(r), kv_rows(r), kv_send.at[kv_count[0]], kv_recv.at[r], sibling)
    kv_count[0] += 1
    for cp in loads[5:8]:
        cp.wait()
    send(w.at[0], w.at[1], w_sem.at[0], w_sem.at[1], sibling)
    for h in range(count):
        gather(h, 1)
    r_across = red_of(1 - xh, y, c)
    arrived(kv_rows(r_across), kv_recv.at[r_across])
    for d in (1, 3, 2):
        kv_send_to(r_across, (b, red_of(xh, y + d, c)))
    for h in range(count):
        gather(h, 2)
    kv_send_to(r_across, sibling)
    for h in range(count):
        gather(h, 3)
    gather(0, 4)
    for h in range(count):
        gather(h, 5)
        if h + 1 < count:
            gather(h + 1, 4)
        gather(h, 6)
        if h == 0:
            arrived(w.at[1], w_sem.at[1])
        project(h)
        send_queries(h, range(7 if h + 1 < count else EARLY))

    def turn(h, v):
        rows = extent[h]
        return (v * cos_ref[rows] + pltpu.roll(v, HD // 2, 1) * sin_ref[rows]).astype(BF16)

    for h in range(count):
        new = pp[h][chip, :, WIDE:PROJ]
        for p, _ in others:
            arrived(kr[h].at[p], kr_recv[h].at[p])
            new = new + restore(kr[h].at[p], size[h] // 16, 2)
        fresh = pl.ds(pl.multiple_of(CACHE + r * ROWS + PIECES[h][0], 16), size[h])
        kv[fresh, 0:HD] = turn(h, new[:, 0:HD])
        kv[fresh, HD : 2 * HD] = new[:, HD : 2 * HD].astype(BF16)

    def nk_rows(red):
        return kv.at[pl.ds(pl.multiple_of(CACHE + red * ROWS, ROWS), ROWS), 0 : 2 * HD]

    def nk_to(slot, red, to):
        send(nk_rows(red), nk_rows(red), nk_send.at[slot], nk_recv.at[red], to)

    for i, (p, to) in enumerate(others):
        nk_to(i, r, to)
    nk_to(7, r, sibling)
    send_queries(count - 1, range(EARLY, 7))

    for red in (
        red_of(xh, y + 1, c), red_of(xh, y + 3, c), red_of(xh, y + 2, c),
        red_of(1 - xh, y + 1, c), red_of(1 - xh, y + 3, c), red_of(1 - xh, y + 2, c),
    ):
        arrived(kv_rows(red), kv_recv.at[red])
        kv_send_to(red, sibling)

    for k in range(8):
        red = rem(chip + k, 8) * 2 + 1 - c
        arrived(kv_rows(red), kv_recv.at[red])
    turn_log = HD ** (-0.5) * math.log2(math.e)

    def scores(h, n):
        keys = kv[pl.ds(pl.multiple_of(n * CHUNK, CHUNK), CHUNK), 0:HD]
        return lax.dot_general(qh[h][...], keys, (((1,), (1,)), ((), ())), preferred_element_type=F32)

    def keep(h, n, t, top):
        s_ref[h][:, pl.ds(pl.multiple_of(n * CHUNK, CHUNK), CHUNK)] = t
        for k in range(CHUNK // HD):
            top = jnp.maximum(top, t[:, k * HD : (k + 1) * HD])
        return top

    def first_pass(h):
        query = pp[h][chip, :, 0:WIDE]
        for p, _ in others:
            arrived(qr[h].at[p], qr_recv[h].at[p])
            query = query + restore(qr[h].at[p], size[h] // 16, 8)
        for k in range(8):
            qh[h][k * size[h] : (k + 1) * size[h], :] = turn(h, query[:, k * HD : (k + 1) * HD])

        def plain(n, top, h=h):
            return keep(h, n, scores(h, n), top)

        def partly(n, top, h=h):
            slot = n * CHUNK + lax.broadcasted_iota(I32, (1, CHUNK), 1)
            return keep(h, n, scores(h, n) + jnp.where(slot < start, 0.0, NEG), top)

        top = jnp.full((8 * size[h], HD), NEG, F32)
        top = lax.fori_loop(0, 4, plain, top)
        return lax.fori_loop(4, 8, partly, top)

    tops = [first_pass(0)]

    for i, (p, _) in enumerate(nearest):
        red = p * 2 + c
        arrived(nk_rows(red), nk_recv.at[red])
        nk_to(8 + i, red, sibling)
    for k in range(8):
        red = rem(chip + k, 8) * 2 + 1 - c
        arrived(nk_rows(red), nk_recv.at[red])

    at_count = [0] * count

    def at_to(h, red, to):
        send(att[h].at[red], att[h].at[red], at_send[h].at[at_count[h]], at_recv[h].at[red], to)
        at_count[h] += 1

    for h in range(count):
        many = 8 * size[h]
        if h > 0:
            tops.append(first_pass(h))
        token = r * ROWS + PIECES[h][0] + rem(lax.broadcasted_iota(I32, (many, CHUNK), 0), size[h])
        ahead = lax.broadcasted_iota(I32, (many, CHUNK), 1) > token
        top = keep(h, 8, jnp.where(ahead, NEG, scores(h, 8)), tops[h])
        peak = jnp.broadcast_to(jnp.max(top, axis=1, keepdims=True), (many, HD))

        mix[h][...] = jnp.zeros((many, 2 * HD), F32)

        def weigh(n, _, h=h, peak=peak):
            base = n * CHUNK
            parts = []
            for k in range(CHUNK // HD):
                t = s_ref[h][:, pl.ds(pl.multiple_of(base + k * HD, HD), HD)]
                parts.append(jnp.exp2((t - peak) * turn_log).astype(BF16))
            wts = jnp.concatenate(parts, axis=1)
            vals = kv[pl.ds(pl.multiple_of(base, CHUNK), CHUNK), HD : 3 * HD]
            mix[h][...] += jnp.dot(wts, vals, preferred_element_type=F32)
            return 0

        lax.fori_loop(0, 9, weigh, 0)
        done = (mix[h][:, 0:HD] / mix[h][:, HD : 2 * HD]).astype(BF16)
        for k in range(8):
            att[h][r, :, k * HD : (k + 1) * HD] = done[k * size[h] : (k + 1) * size[h], :]
        for p, to in others:
            at_to(h, r, to)
        at_to(h, r, sibling)
    sent(sends[-16:])

    loads[8].wait()

    def project_out(h):
        for p, _ in nearest:
            red = p * 2 + c
            arrived(att[h].at[red], at_recv[h].at[red])
            at_to(h, red, sibling)
        for k in range(8):
            red = rem(chip + k, 8) * 2 + 1 - c
            arrived(att[h].at[red], at_recv[h].at[red])
        for m in range(2):
            x = att[h][m * 8 : (m + 1) * 8].reshape(8 * size[h], WIDE)
            for n in range(WIDE // 256):
                lanes = slice(n * 256, (n + 1) * 256)
                t = jnp.dot(x, wo[:, lanes], preferred_element_type=F32)
                op[h][m * 8 : (m + 1) * 8, :, lanes] = t.reshape(8, size[h], 256)

    def ring(h, stage):
        s = sense[h]
        up, down, over = z_next[s], z_next[-s], z_over[s]

        def own(d):
            return op[h][blk_of(xl, z + s * d)]

        def other(d):
            return op[h][blk_of(ox, z + s * d)]

        def x_send(k, v):
            quantize(xs[h].at[k], v)
            send(xs[h].at[k], xr[h].at[k], xs_send[h].at[k], xr_recv[h].at[k], x_pair)

        def x_get(k):
            arrived(xr[h].at[k], xr_recv[h].at[k])
            return restore(xr[h].at[k], size[h] // 16, 8)

        def z_send(k, v, to):
            quantize(zs[h].at[k], v)
            send(zs[h].at[k], zr[h].at[k], zs_send[h].at[k], zr_recv[h].at[k], to)

        def z_get(k):
            arrived(zr[h].at[k], zr_recv[h].at[k])
            return restore(zr[h].at[k], size[h] // 16, 8)

        if stage == 0:
            x_send(0, other(4))
            z_send(9, other(-2), down)
            x_send(1, other(-3))
            x_send(2, other(3))
            x_send(4, other(2))
        if stage == 1:
            z_send(0, own(4) + x_get(0), up)
            z_send(6, own(-3) + x_get(1), down)
            z_send(5, other(1), up)
        if stage == 2:
            z_send(10, other(-1) + z_get(9), down)
        if stage == 3:
            z_send(1, own(3) + z_get(0) + x_get(2), up)
            z_send(7, own(-2) + z_get(6), down)
        if stage == 4:
            x_send(3, other(0) + z_get(5) + z_get(10))
        if stage == 5:
            z_send(2, own(2) + z_get(1) + x_get(4), up)
            z_send(8, own(-1) + z_get(7), down)
        if stage == 6:
            z_send(3, own(1) + z_get(2), up)
        if stage == 7:
            rows = extent[h]
            out_ref[rows] = res[rows] + (own(0) + x_get(3) + z_get(8) + z_get(3))

    for step in (9, 0, 1, 2, 19, 10, 3, 11, 12, 4, 5, 13, 6, 14, 15, 7, 16, 17):
        if step % 10 == 9:
            project_out(step // 10)
        else:
            ring(step // 10, step % 10)
    sent([])


def on_device(resid, norm_gain, w_query, w_key, w_value, w_out, cache_key, cache_value, prefix_len):
    half = HD // 2
    steps = jnp.arange(HD, dtype=I32)
    steps = jnp.where(steps < half, steps, steps - half).astype(F32)
    freq = (THETA ** (-(steps * 2.0) / HD))[None, :]
    vmem = pl.BlockSpec(memory_space=pltpu.VMEM)
    hbm = pl.BlockSpec(memory_space=pl.ANY)
    dma = pltpu.SemaphoreType.DMA
    scratch = [
        pltpu.VMEM((ROWS, HD), F32),
        pltpu.VMEM((ROWS, HD), F32),
        pltpu.VMEM((ROWS, WIDE), F32),
        pltpu.VMEM((2, WIDE, PROJ), BF16),
        pltpu.VMEM((WIDE, WIDE), BF16),
        pltpu.VMEM((KEYS, 3 * HD), BF16),
        pltpu.VMEM((SLOTS, 2 * HD), BF16),
        pltpu.VMEM((16, 8, HD), F32),
        dma((9,)), dma((2,)), dma((15,)), dma((16,)),
        dma((15,)), dma((16,)), dma((15,)), dma((16,)),
    ]
    for _, n in PIECES:
        few, many = (tiles(n, 2 * HD), 16, HD), (tiles(n, WIDE), 16, HD)
        scratch += [
            pltpu.VMEM((2, 8, n, WIDE), BF16),
            pltpu.VMEM((8, n, WIDE), BF16),
            pltpu.VMEM((8, n, PROJ), F32),
            pltpu.VMEM((7,) + few, I16),
            pltpu.VMEM((8,) + few, I16),
            pltpu.VMEM((7,) + many, I16),
            pltpu.VMEM((8,) + many, I16),
            pltpu.VMEM((8 * n, HD), BF16),
            pltpu.VMEM((8 * n, KEYS), F32),
            pltpu.VMEM((8 * n, 2 * HD), F32),
            pltpu.VMEM((16, n, WIDE), BF16),
            pltpu.VMEM((16, n, WIDE), F32),
            pltpu.VMEM((5,) + many, I16),
            pltpu.VMEM((5,) + many, I16),
            pltpu.VMEM((11,) + many, I16),
            pltpu.VMEM((11,) + many, I16),
            dma((15,)), dma((16,)), dma((8,)), dma((8,)),
            dma((7,)), dma((8,)), dma((7,)), dma((8,)),
            dma((15,)), dma((16,)),
            dma((5,)), dma((5,)), dma((11,)), dma((11,)),
        ]
    return pl.pallas_call(
        kernel,
        out_shape=jax.ShapeDtypeStruct((ROWS, WIDE), F32),
        in_specs=[pl.BlockSpec(memory_space=pltpu.SMEM), hbm, vmem, hbm, hbm, hbm, hbm, hbm, hbm, vmem],
        out_specs=vmem,
        scratch_shapes=scratch,
        compiler_params=pltpu.CompilerParams(
            collective_id=0, has_side_effects=True, vmem_limit_bytes=58 * 1024 * 1024
        ),
    )(prefix_len, resid, norm_gain[None, :], w_query, w_key, w_value, w_out, cache_key, cache_value, freq)


def solution(mesh):
    placed = (
        P("blk", "red"), P("red"), P("red", "blk"), P("red", None), P("red", None), P("blk", "red"),
        P("red", None), P("red", None), P(),
    )
    return jax.shard_map(on_device, mesh=mesh, in_specs=placed, out_specs=P("blk", "red"), check_vma=False)
```

```python
import functools
import math

import jax
import jax.numpy as jnp
from jax import lax
from jax.experimental import pallas as pl
from jax.experimental.pallas import tpu as pltpu
from jax.sharding import PartitionSpec as P

MESH = pl.DeviceIdType.MESH
F32, BF16, I16, I32 = jnp.float32, jnp.bfloat16, jnp.int16, jnp.int32

HD = 128
THETA = 500000.0
ROWS = 64
WIDE = 1024
PROJ = WIDE + 2 * HD
SLOTS = 512
CACHE = 8192
SPAN = 1024
KEYS = CACHE + SPAN
CHUNK = 1024
PIECES = ((0, 32), (32, 32))
EARLY = 4
LANES = 32
STEP = 8.0
TOP = 32000.0
NEG = -1e30


def rem(a, n):
    return lax.rem(a, jnp.int32(n))


def tiles(rows, lanes):
    return rows // 16 * (lanes // HD) + 1


def quantize(dst, v):
    wide, groups = v.shape[1] // HD, v.shape[0] // 16
    lane = lax.broadcasted_iota(I32, (16, HD), 1)
    exponents = jnp.zeros((16, HD), F32)
    for m in range(groups):
        rows = v[m * 16 : (m + 1) * 16]
        fold = jnp.abs(rows[:, :HD])
        for k in range(1, wide):
            fold = jnp.maximum(fold, jnp.abs(rows[:, k * HD : (k + 1) * HD]))
        top = jnp.max(fold, axis=1, keepdims=True)
        e = jnp.broadcast_to(jnp.ceil(jnp.log2(jnp.maximum(top, 1e-30)) * STEP), (16, HD))
        exponents = e if m == 0 else jnp.where(lane < m * LANES, exponents, e)
        up = jnp.exp2(e * (-1.0 / STEP)) * TOP
        for k in range(wide):
            dst[m * wide + k] = jnp.round(rows[:, k * HD : (k + 1) * HD] * up).astype(I32).astype(I16)
    dst[groups * wide] = exponents.astype(I32).astype(I16)


def restore(src, groups, wide):
    e = src[groups * wide].astype(I32).astype(F32)
    parts = []
    for m in range(groups):
        lane = m * LANES
        down = jnp.broadcast_to(jnp.exp2(e[:, lane : lane + 1] * (1.0 / STEP)) * (1.0 / TOP), (16, HD))
        parts.append(
            jnp.concatenate([src[m * wide + k].astype(I32).astype(F32) * down for k in range(wide)], axis=1)
        )
    return jnp.concatenate(parts, axis=0)


def kernel(
    start_ref, resid_hbm, gain_ref, wq_hbm, wk_hbm, wv_hbm, wo_hbm, ck_hbm, cv_hbm, freq_ref,
    out_ref,
    cos_ref, sin_ref, res, w, wo, kv, pb, sq,
    load_sem, w_sem, sq_send, sq_recv, kv_send, kv_recv, nk_send, nk_recv,
    *per_piece,
):
    (
        g, gs, pp, ks, kr, qs, qr, qh, s_ref, mix,
        att, op, xs, xr, zs, zr,
        ag_send, ag_recv, gs_send, gs_recv, ks_send, kr_recv, qs_send, qr_recv,
        at_send, at_recv, xs_send, xr_recv, zs_send, zr_recv,
    ) = [per_piece[k :: 30] for k in range(30)]
    count = len(PIECES)
    sense = [1 - 2 * (h % 2) for h in range(count)]
    extent = [slice(first, first + rows) for first, rows in PIECES]
    size = [rows for _, rows in PIECES]
    b = lax.axis_index("blk")
    r = lax.axis_index("red")
    xl, z = lax.div(b, jnp.int32(8)), rem(b, 8)
    xh, y, c = lax.div(r, jnp.int32(8)), rem(lax.div(r, jnp.int32(2)), 4), rem(r, 2)
    chip = lax.div(r, jnp.int32(2))
    head = lax.div(b, jnp.int32(2))
    ox = 1 - xl

    def blk_of(px, pz):
        return px * 8 + rem(pz + 16, 8)

    def red_of(px, py, pc):
        return (px * 4 + rem(py + 8, 4)) * 2 + pc

    z_next = {1: (blk_of(xl, z + 1), r), -1: (blk_of(xl, z - 1), r)}
    z_over = {1: (blk_of(xl, z + 2), r), -1: (blk_of(xl, z - 2), r)}
    x_pair = (blk_of(ox, z), r)
    x_across = (blk_of(ox, z), red_of(1 - xh, y, c))
    sibling = (b, red_of(xh, y, 1 - c))
    others = []
    for dx, dy in ((1, 2), (0, 1), (1, 0), (0, 3), (1, 1), (0, 2), (1, 3)):
        p = lax.div(red_of(rem(xh + dx, 2), y + dy, 0), jnp.int32(2))
        others.append((p, (b, p * 2 + c)))

    nearest = [others[i] for i in (1, 3, 2, 5, 4, 6, 0)]

    barrier = pltpu.get_barrier_semaphore()
    peers = [(b, rem(r + i, 16)) for i in range(1, 16)] + [z_next[1], z_next[-1], z_over[1], z_over[-1], x_pair, x_across]
    for p in peers:
        pl.semaphore_signal(barrier, inc=1, device_id=p, device_id_type=MESH)

    mine = pl.ds(pl.multiple_of(r * SLOTS, SLOTS), SLOTS)
    my_cols = pl.ds(pl.multiple_of(head * HD, HD), HD)
    pair_head = lax.div(blk_of(ox, z), jnp.int32(2))
    pair_cols = pl.ds(pl.multiple_of(pair_head * HD, HD), HD)
    loads = [
        pltpu.make_async_copy(resid_hbm, res, load_sem.at[0]),
        pltpu.make_async_copy(ck_hbm.at[:, my_cols], kv.at[mine, 0:HD], load_sem.at[1]),
        pltpu.make_async_copy(cv_hbm.at[:, my_cols], kv.at[mine, HD : 2 * HD], load_sem.at[2]),
        pltpu.make_async_copy(ck_hbm.at[:, pair_cols], pb.at[:, 0:HD], load_sem.at[3]),
        pltpu.make_async_copy(cv_hbm.at[:, pair_cols], pb.at[:, HD : 2 * HD], load_sem.at[4]),
        pltpu.make_async_copy(wq_hbm, w.at[0, :, 0:WIDE], load_sem.at[5]),
        pltpu.make_async_copy(wk_hbm.at[:, my_cols], w.at[0, :, WIDE : WIDE + HD], load_sem.at[6]),
        pltpu.make_async_copy(wv_hbm.at[:, my_cols], w.at[0, :, WIDE + HD : PROJ], load_sem.at[7]),
        pltpu.make_async_copy(wo_hbm, wo, load_sem.at[8]),
    ]
    for cp in loads:
        cp.start()

    sends = []

    def send(src, dst, ssem, rsem, to):
        cp = pltpu.make_async_remote_copy(
            src_ref=src, dst_ref=dst, send_sem=ssem, recv_sem=rsem, device_id=to, device_id_type=MESH
        )
        cp.start()
        sends.append(cp)

    def sent(keep):
        for cp in sends[: len(sends) - len(keep)]:
            cp.wait_send()
        sends[:] = list(keep)

    def arrived(dst, rsem):
        pltpu.make_async_remote_copy(
            src_ref=dst, dst_ref=dst, send_sem=load_sem.at[0], recv_sem=rsem, device_id=sibling, device_id_type=MESH
        ).wait_recv()

    kv[:, 2 * HD : 3 * HD] = jnp.ones((KEYS, HD), BF16)

    start = start_ref[0]
    position = (start + r * ROWS + lax.broadcasted_iota(I32, (ROWS, HD), 0)).astype(F32)
    angle = position * freq_ref[...]
    first = lax.broadcasted_iota(I32, (ROWS, HD), 1) < HD // 2
    cos_ref[...] = jnp.cos(angle)
    sine = jnp.sin(angle)
    sin_ref[...] = jnp.where(first, -sine, sine)

    loads[0].wait()
    fold = jnp.zeros((ROWS, HD), F32)
    for k in range(WIDE // HD):
        v = res[:, k * HD : (k + 1) * HD]
        fold = fold + v * v
    square = jnp.concatenate([fold, jnp.zeros((HD - ROWS, HD), F32)], axis=0).T
    sq[r] = jnp.broadcast_to(jnp.sum(square, axis=0, keepdims=True), (8, HD))
    pl.semaphore_wait(barrier, len(peers))
    for i, (p, to) in enumerate(others):
        send(sq.at[r], sq.at[r], sq_send.at[2 * i], sq_recv.at[r], to)
        send(sq.at[r], sq.at[r], sq_send.at[2 * i + 1], sq_recv.at[r], (b, p * 2 + 1 - c))
    send(sq.at[r], sq.at[r], sq_send.at[14], sq_recv.at[r], sibling)

    for cp in loads[1:5]:
        cp.wait()

    def kv_rows(red):
        return kv.at[pl.ds(pl.multiple_of(red * SLOTS, SLOTS), SLOTS), 0 : 2 * HD]

    kv_count = [0]

    def kv_send_to(red, to, src=None):
        send(kv_rows(red) if src is None else src, kv_rows(red), kv_send.at[kv_count[0]], kv_recv.at[red], to)
        kv_count[0] += 1

    kv_send_to(r, x_across, src=pb)
    for d in (1, 3, 2):
        kv_send_to(r, (b, red_of(xh, y + d, c)))

    for i in range(1, 16):
        p = rem(r + i, 16)
        arrived(sq.at[p], sq_recv.at[p])
    total = jnp.sum(sq[...], axis=0)[0:1]
    column = jnp.broadcast_to(total, (HD, HD)).T[:ROWS]
    factor = lax.rsqrt(column / (WIDE * 16.0) + 1e-05)
    gain = gain_ref[...]

    def g_at(h, px, pz):
        pz = rem(pz + 16, 8)
        return g[h].at[rem(pz, 2), px * 4 + lax.div(pz, jnp.int32(2))]

    ag_count = [0] * count

    def g_wait(h, px, d):
        pz = z + sense[h] * d
        arrived(g_at(h, px, pz), ag_recv[h].at[blk_of(px, pz)])

    def g_send(h, px, d, *to):
        pz = z + sense[h] * d
        for t in to:
            s = sense[h] * t
            device = {0: x_pair, 1: z_next.get(s), 2: z_over.get(s // 2)}[abs(t)]
            send(g_at(h, px, pz), g_at(h, px, pz), ag_send[h].at[ag_count[h]], ag_recv[h].at[blk_of(px, pz)], device)
            ag_count[h] += 1

    gs_count = [0] * count

    def g_trade(h, px, d, e):
        s = sense[h]
        pz = rem(z + 16 + jnp.where(rem(z + 16 + s * d, 2) == 1 - c, s * d, s * e), 8)
        j = px * 4 + lax.div(pz, jnp.int32(2))
        send(g[h].at[1 - c, j], gs[h].at[j], gs_send[h].at[gs_count[h]], gs_recv[h].at[j], sibling)
        gs_count[h] += 1

    def gather(h, stage):
        if stage == 0:
            rows = extent[h]
            slot = g_at(h, xl, z)
            for k in range(WIDE // HD):
                lanes = slice(k * HD, (k + 1) * HD)
                slot[:, lanes] = (res[rows, lanes] * factor[rows] * gain[:, lanes]).astype(BF16)
            g_send(h, xl, 0, 1, -1, 0)
        if stage == 1:
            g_wait(h, xl, -1)
            g_send(h, xl, -1, 1)
            g_wait(h, xl, 1)
            g_send(h, xl, 1, -1)
            g_wait(h, ox, 0)
            g_send(h, ox, 0, 1, -1)
            g_trade(h, xl, 0, -1)
        if stage == 2:
            g_wait(h, xl, -2)
            g_send(h, xl, -2, 1)
            g_wait(h, xl, 2)
            g_send(h, xl, 2, -1)
            g_wait(h, ox, -1)
            g_send(h, ox, -1, 1)
            g_wait(h, ox, 1)
            g_send(h, ox, 1, -1)
            g_trade(h, xl, 1, -2)
            g_trade(h, ox, 0, -1)
        if stage == 3:
            g_wait(h, xl, -3)
            g_send(h, xl, -3, 1, 0)
            g_wait(h, xl, 3)
            g_send(h, xl, 3, 0)
            g_trade(h, xl, 2, -3)
        if stage == 4:
            g_wait(h, xl, -4)
            g_send(h, xl, -4, 0)
            g_trade(h, xl, 3, -4)
        if stage == 5:
            g_wait(h, ox, -2)
            g_wait(h, ox, 2)
            g_trade(h, ox, 1, -2)
            g_wait(h, ox, -3)
            g_wait(h, ox, 3)
            g_trade(h, ox, 2, -3)
        if stage == 6:
            g_wait(h, ox, -4)
            g_trade(h, ox, 3, -4)
            for j in range(8):
                arrived(gs[h].at[j], gs_recv[h].at[j])

    def project(h):
        x0 = g[h].at[c][...].reshape(8 * size[h], WIDE)
        x1 = gs[h][...].reshape(8 * size[h], WIDE)

        def columns(n):
            lanes = slice(n * 256, (n + 1) * 256)
            t = jnp.dot(x0, w[0, :, lanes], preferred_element_type=F32)
            t = t + jnp.dot(x1, w[1, :, lanes], preferred_element_type=F32)
            pp[h][:, :, lanes] = t.reshape(8, size[h], 256)

        columns(WIDE // 256)
        for i, (p, to) in enumerate(others):
            quantize(ks[h].at[i], pp[h][p, :, WIDE:PROJ])
            send(ks[h].at[i], kr[h].at[chip], ks_send[h].at[i], kr_recv[h].at[chip], to)
        for n in range(WIDE // 256):
            columns(n)

    def send_queries(h, which):
        for i in which:
            p, to = others[i]
            quantize(qs[h].at[i], pp[h][p, :, 0:WIDE])
            send(qs[h].at[i], qr[h].at[chip], qs_send[h].at[i], qr_recv[h].at[chip], to)

    for h in range(count):
        gather(h, 0)
    send(kv_rows(r), kv_rows(r), kv_send.at[kv_count[0]], kv_recv.at[r], sibling)
    kv_count[0] += 1
    for cp in loads[5:8]:
        cp.wait()
    send(w.at[0], w.at[1], w_sem.at[0], w_sem.at[1], sibling)
    for h in range(count):
        gather(h, 1)
    r_across = red_of(1 - xh, y, c)
    arrived(kv_rows(r_across), kv_recv.at[r_across])
    for d in (1, 3, 2):
        kv_send_to(r_across, (b, red_of(xh, y + d, c)))
    for h in range(count):
        gather(h, 2)
    kv_send_to(r_across, sibling)
    for h in range(count):
        gather(h, 3)
    gather(0, 4)
    for h in range(count):
        gather(h, 5)
        if h + 1 < count:
            gather(h + 1, 4)
        gather(h, 6)
        if h == 0:
            arrived(w.at[1], w_sem.at[1])
        project(h)
        send_queries(h, range(7 if h + 1 < count else EARLY))

    def turn(h, v):
        rows = extent[h]
        return (v * cos_ref[rows] + pltpu.roll(v, HD // 2, 1) * sin_ref[rows]).astype(BF16)

    for h in range(count):
        new = pp[h][chip, :, WIDE:PROJ]
        for p, _ in others:
            arrived(kr[h].at[p], kr_recv[h].at[p])
            new = new + restore(kr[h].at[p], size[h] // 16, 2)
        fresh = pl.ds(pl.multiple_of(CACHE + r * ROWS + PIECES[h][0], 16), size[h])
        kv[fresh, 0:HD] = turn(h, new[:, 0:HD])
        kv[fresh, HD : 2 * HD] = new[:, HD : 2 * HD].astype(BF16)

    def nk_rows(red):
        return kv.at[pl.ds(pl.multiple_of(CACHE + red * ROWS, ROWS), ROWS), 0 : 2 * HD]

    def nk_to(slot, red, to):
        send(nk_rows(red), nk_rows(red), nk_send.at[slot], nk_recv.at[red], to)

    for i, (p, to) in enumerate(others):
        nk_to(i, r, to)
    nk_to(7, r, sibling)
    send_queries(count - 1, range(EARLY, 7))

    for red in (
        red_of(xh, y + 1, c), red_of(xh, y + 3, c), red_of(xh, y + 2, c),
        red_of(1 - xh, y + 1, c), red_of(1 - xh, y + 3, c), red_of(1 - xh, y + 2, c),
    ):
        arrived(kv_rows(red), kv_recv.at[red])
        kv_send_to(red, sibling)

    for k in range(8):
        red = rem(chip + k, 8) * 2 + 1 - c
        arrived(kv_rows(red), kv_recv.at[red])
    turn_log = HD ** (-0.5) * math.log2(math.e)

    def scores(h, n):
        keys = kv[pl.ds(pl.multiple_of(n * CHUNK, CHUNK), CHUNK), 0:HD]
        return lax.dot_general(qh[h][...], keys, (((1,), (1,)), ((), ())), preferred_element_type=F32)

    def keep(h, n, t, top):
        s_ref[h][:, pl.ds(pl.multiple_of(n * CHUNK, CHUNK), CHUNK)] = t
        for k in range(CHUNK // HD):
            top = jnp.maximum(top, t[:, k * HD : (k + 1) * HD])
        return top

    def first_pass(h):
        query = pp[h][chip, :, 0:WIDE]
        for p, _ in others:
            arrived(qr[h].at[p], qr_recv[h].at[p])
            query = query + restore(qr[h].at[p], size[h] // 16, 8)
        for k in range(8):
            qh[h][k * size[h] : (k + 1) * size[h], :] = turn(h, query[:, k * HD : (k + 1) * HD])

        def plain(n, top, h=h):
            return keep(h, n, scores(h, n), top)

        def partly(n, top, h=h):
            slot = n * CHUNK + lax.broadcasted_iota(I32, (1, CHUNK), 1)
            return keep(h, n, scores(h, n) + jnp.where(slot < start, 0.0, NEG), top)

        top = jnp.full((8 * size[h], HD), NEG, F32)
        top = lax.fori_loop(0, 4, plain, top, unroll=2)
        return lax.fori_loop(4, 8, partly, top, unroll=2)

    tops = [first_pass(0)]

    for i, (p, _) in enumerate(nearest):
        red = p * 2 + c
        arrived(nk_rows(red), nk_recv.at[red])
        nk_to(8 + i, red, sibling)
    for k in range(8):
        red = rem(chip + k, 8) * 2 + 1 - c
        arrived(nk_rows(red), nk_recv.at[red])

    at_count = [0] * count

    def at_to(h, red, to):
        send(att[h].at[red], att[h].at[red], at_send[h].at[at_count[h]], at_recv[h].at[red], to)
        at_count[h] += 1

    for h in range(count):
        many = 8 * size[h]
        if h > 0:
            tops.append(first_pass(h))
        token = r * ROWS + PIECES[h][0] + rem(lax.broadcasted_iota(I32, (many, CHUNK), 0), size[h])
        ahead = lax.broadcasted_iota(I32, (many, CHUNK), 1) > token
        top = keep(h, 8, jnp.where(ahead, NEG, scores(h, 8)), tops[h])
        peak = jnp.broadcast_to(jnp.max(top, axis=1, keepdims=True), (many, HD))

        mix[h][...] = jnp.zeros((many, 2 * HD), F32)

        def weigh(n, _, h=h, peak=peak):
            base = n * CHUNK
            parts = []
            for k in range(CHUNK // HD):
                t = s_ref[h][:, pl.ds(pl.multiple_of(base + k * HD, HD), HD)]
                parts.append(jnp.exp2((t - peak) * turn_log).astype(BF16))
            wts = jnp.concatenate(parts, axis=1)
            vals = kv[pl.ds(pl.multiple_of(base, CHUNK), CHUNK), HD : 3 * HD]
            mix[h][...] += jnp.dot(wts, vals, preferred_element_type=F32)
            return 0

        lax.fori_loop(0, 9, weigh, 0, unroll=3)
        done = (mix[h][:, 0:HD] / mix[h][:, HD : 2 * HD]).astype(BF16)
        for k in range(8):
            att[h][r, :, k * HD : (k + 1) * HD] = done[k * size[h] : (k + 1) * size[h], :]
        for p, to in others:
            at_to(h, r, to)
        at_to(h, r, sibling)
    sent(sends[-16:])

    loads[8].wait()

    def project_out(h):
        for p, _ in nearest:
            red = p * 2 + c
            arrived(att[h].at[red], at_recv[h].at[red])
            at_to(h, red, sibling)
        for k in range(8):
            red = rem(chip + k, 8) * 2 + 1 - c
            arrived(att[h].at[red], at_recv[h].at[red])
        for m in range(2):
            x = att[h][m * 8 : (m + 1) * 8].reshape(8 * size[h], WIDE)
            for n in range(WIDE // 256):
                lanes = slice(n * 256, (n + 1) * 256)
                t = jnp.dot(x, wo[:, lanes], preferred_element_type=F32)
                op[h][m * 8 : (m + 1) * 8, :, lanes] = t.reshape(8, size[h], 256)

    def ring(h, stage):
        s = sense[h]
        up, down, over = z_next[s], z_next[-s], z_over[s]

        def own(d):
            return op[h][blk_of(xl, z + s * d)]

        def other(d):
            return op[h][blk_of(ox, z + s * d)]

        def x_send(k, v):
            quantize(xs[h].at[k], v)
            send(xs[h].at[k], xr[h].at[k], xs_send[h].at[k], xr_recv[h].at[k], x_pair)

        def x_get(k):
            arrived(xr[h].at[k], xr_recv[h].at[k])
            return restore(xr[h].at[k], size[h] // 16, 8)

        def z_send(k, v, to):
            quantize(zs[h].at[k], v)
            send(zs[h].at[k], zr[h].at[k], zs_send[h].at[k], zr_recv[h].at[k], to)

        def z_get(k):
            arrived(zr[h].at[k], zr_recv[h].at[k])
            return restore(zr[h].at[k], size[h] // 16, 8)

        if stage == 0:
            x_send(0, other(4))
            z_send(9, other(-2), down)
            x_send(1, other(-3))
            x_send(2, other(3))
            x_send(4, other(2))
        if stage == 1:
            z_send(0, own(4) + x_get(0), up)
            z_send(6, own(-3) + x_get(1), down)
            z_send(5, other(1), up)
        if stage == 2:
            z_send(10, other(-1) + z_get(9), down)
        if stage == 3:
            z_send(1, own(3) + z_get(0) + x_get(2), up)
            z_send(7, own(-2) + z_get(6), down)
        if stage == 4:
            x_send(3, other(0) + z_get(5) + z_get(10))
        if stage == 5:
            z_send(2, own(2) + z_get(1) + x_get(4), up)
            z_send(8, own(-1) + z_get(7), down)
        if stage == 6:
            z_send(3, own(1) + z_get(2), up)
        if stage == 7:
            rows = extent[h]
            out_ref[rows] = res[rows] + (own(0) + x_get(3) + z_get(8) + z_get(3))

    for step in (9, 0, 1, 2, 19, 10, 3, 11, 12, 4, 5, 13, 6, 14, 15, 7, 16, 17):
        if step % 10 == 9:
            project_out(step // 10)
        else:
            ring(step // 10, step % 10)
    sent([])


def on_device(resid, norm_gain, w_query, w_key, w_value, w_out, cache_key, cache_value, prefix_len):
    half = HD // 2
    steps = jnp.arange(HD, dtype=I32)
    steps = jnp.where(steps < half, steps, steps - half).astype(F32)
    freq = (THETA ** (-(steps * 2.0) / HD))[None, :]
    vmem = pl.BlockSpec(memory_space=pltpu.VMEM)
    hbm = pl.BlockSpec(memory_space=pl.ANY)
    dma = pltpu.SemaphoreType.DMA
    scratch = [
        pltpu.VMEM((ROWS, HD), F32),
        pltpu.VMEM((ROWS, HD), F32),
        pltpu.VMEM((ROWS, WIDE), F32),
        pltpu.VMEM((2, WIDE, PROJ), BF16),
        pltpu.VMEM((WIDE, WIDE), BF16),
        pltpu.VMEM((KEYS, 3 * HD), BF16),
        pltpu.VMEM((SLOTS, 2 * HD), BF16),
        pltpu.VMEM((16, 8, HD), F32),
        dma((9,)), dma((2,)), dma((15,)), dma((16,)),
        dma((15,)), dma((16,)), dma((15,)), dma((16,)),
    ]
    for _, n in PIECES:
        few, many = (tiles(n, 2 * HD), 16, HD), (tiles(n, WIDE), 16, HD)
        scratch += [
            pltpu.VMEM((2, 8, n, WIDE), BF16),
            pltpu.VMEM((8, n, WIDE), BF16),
            pltpu.VMEM((8, n, PROJ), F32),
            pltpu.VMEM((7,) + few, I16),
            pltpu.VMEM((8,) + few, I16),
            pltpu.VMEM((7,) + many, I16),
            pltpu.VMEM((8,) + many, I16),
            pltpu.VMEM((8 * n, HD), BF16),
            pltpu.VMEM((8 * n, KEYS), F32),
            pltpu.VMEM((8 * n, 2 * HD), F32),
            pltpu.VMEM((16, n, WIDE), BF16),
            pltpu.VMEM((16, n, WIDE), F32),
            pltpu.VMEM((5,) + many, I16),
            pltpu.VMEM((5,) + many, I16),
            pltpu.VMEM((11,) + many, I16),
            pltpu.VMEM((11,) + many, I16),
            dma((15,)), dma((16,)), dma((8,)), dma((8,)),
            dma((7,)), dma((8,)), dma((7,)), dma((8,)),
            dma((15,)), dma((16,)),
            dma((5,)), dma((5,)), dma((11,)), dma((11,)),
        ]
    return pl.pallas_call(
        kernel,
        out_shape=jax.ShapeDtypeStruct((ROWS, WIDE), F32),
        in_specs=[pl.BlockSpec(memory_space=pltpu.SMEM), hbm, vmem, hbm, hbm, hbm, hbm, hbm, hbm, vmem],
        out_specs=vmem,
        scratch_shapes=scratch,
        compiler_params=pltpu.CompilerParams(
            collective_id=0, has_side_effects=True, vmem_limit_bytes=58 * 1024 * 1024
        ),
    )(prefix_len, resid, norm_gain[None, :], w_query, w_key, w_value, w_out, cache_key, cache_value, freq)


def solution(mesh):
    placed = (
        P("blk", "red"), P("red"), P("red", "blk"), P("red", None), P("red", None), P("blk", "red"),
        P("red", None), P("red", None), P(),
    )
    return jax.shard_map(on_device, mesh=mesh, in_specs=placed, out_specs=P("blk", "red"), check_vma=False)
```
